32 devices in a mesh: seq: 8 (over z, y), tp: 4 (over x, core).
Axes of the slice: x: 2, y: 2, z: 4, core: 2. Of those that a mesh axis runs over, the one named last changes fastest.
Arguments:
- queries: bfloat16 [1536, 2048], P('seq', 'tp'), may hold values from -6 to 6
- keys: bfloat16 [1536, 2048], P('seq', 'tp'), may hold values from -6 to 6
- values: bfloat16 [1536, 2048], P('seq', 'tp'), may hold values from -6 to 6
- lengths: int32 [4], replicated, may hold values from 1 to 768, 1536 in all
- resid: bfloat16 [1536, 2048], P(('seq', 'tp')), may hold values from -6 to 6
- w_out: bfloat16 [2048, 2048], P('tp'), may hold values from -0.5 to 0.5
- moe_gain: float32 [2048], replicated, may hold values from 0.25 to 1.75
- routes: int32 [1536, 8], P(('seq', 'tp')), may hold values from 0 to 15, all different within a row; in each aligned block of 48 rows (0 to 47, 48 to 95, ...) at most 36 rows name the same one
- gates: float32 [1536, 8], P(('seq', 'tp')), may hold values from 0.05 to 0.3
- w_gate_up: bfloat16 [16, 2048, 2, 1024], P('seq', None, None, 'tp'), may hold values from -0.125 to 0.125
- w_down: bfloat16 [16, 1024, 2048], P('seq', 'tp'), may hold values from -0.1875 to 0.1875
Outputs:
- attended: bfloat16 [1536, 2048], P(('seq', 'tp'))
- expert_mix: bfloat16 [1536, 2048], P(('seq', 'tp'))
The draws below stay inside these ranges and needn't reach their ends.
Inputs may be any that keep to these rules, and one draw needn't show every extreme that they name: The 4 lengths sum to 1536; the largest is exactly 768. `routes`: each row names 8 different experts. Within each aligned block of 48 rows (the rows of one device) no expert is named by more than 36 rows, a bound that some block reaches.
All inputs are finite; a program needn't handle non-finite values.
Results may differ from the reference program's by a relative error of at most 0.03.
Values may be sent and summed in bfloat16 or wider, within the bound.
No kernel may reach another device: no remote copies, remote signals or barrier semaphores. Data moves between devices by JAX's collectives and lax.ppermute only.
A program may use at most 128 MiB of HBM per device.

```python
import math
import jax
import jax.numpy as jnp
import numpy as np
from jax import lax

D = 2048
HEADS = 16
HEAD_DIM = 128
FF = 1024
TOP = 8
TENANTS = 4
EXPERTS = 16
TOKENS = 1536
ROWS_DEV = 48
CAP = 36
N_TP = 4


def base_field(key):
    return jax.random.truncated_normal(key, -6.0, 6.0, (TOKENS, HEADS * HEAD_DIM), jnp.float32)


def draw_queries(key, part):
    field = base_field(jax.random.fold_in(key, 1))
    return field.astype(jnp.bfloat16)


def draw_keys(key, part):
    field = base_field(jax.random.fold_in(key, 2))
    return field.astype(jnp.bfloat16)


def levels(rng, extent, shards, smallest, top_value):
    factor_of = 1.0
    for dim, blocks in shards:
        heights = jax.random.uniform(jax.random.fold_in(jax.random.fold_in(rng, 6), dim), (blocks,), jnp.float32, smallest / len(shards), top_value / len(shards))
        factor_of = factor_of * jnp.repeat(jnp.exp(heights), extent[dim] // blocks).reshape((-1,) + (1,) * (len(extent) - 1 - dim))
    return factor_of


def length_profile(count, total, bound, lean):
    loads = [(1 << 20) // math.isqrt(rank ** lean) + 1 for rank in range(2, count + 1)]
    spare, holding = total - bound - (count - 1), [1] * (count - 1)
    while spare > 0:
        candidates = [i for i in range(count - 1) if holding[i] < bound]
        pool, remaining = sum([loads[i] for i in candidates]), spare
        for i in candidates:
            extra = min(bound - holding[i], max(1, remaining * loads[i] // pool), spare)
            holding[i] = holding[i] + extra
            spare = spare - extra
    return np.array([bound] + holding)


def ragged_sizes(own_key, number_of, total, reach, slope):
    if number_of == 2:
        one = jax.random.randint(own_key, (), max(1, total - reach), min(reach, total - 1) + 1)
        return jnp.stack([one, total - one])
    sizes = jnp.asarray(length_profile(number_of, total, reach, slope), jnp.int32)
    couples = (number_of - 1) // 2
    giver, taker = sizes[1:1 + 2 * couples:2], sizes[2:2 + 2 * couples:2]
    room = jnp.minimum(giver - 1, reach - taker)
    shifted = jax.random.randint(jax.random.fold_in(own_key, 1), (couples,), 0, 1 << 20) % (room + 1)
    sizes = sizes.at[1:1 + 2 * couples:2].set(giver - shifted).at[2:2 + 2 * couples:2].set(taker + shifted)
    return sizes[jax.random.permutation(jax.random.fold_in(own_key, 2), number_of)]


def assign_block(stream_key, own, number, rows, amount, top, most, skew):
    sequence = jax.random.permutation(stream_key, amount)
    packed, usual = portions_of(amount, rows * top, most, skew, True), portions_of(amount, rows * top, most, skew, False)
    places = jnp.arange(amount)

    def named(tallies, offset_by):
        used = int((tallies > 0).sum())
        fixed = max(1, used // 4)
        passed = fixed + (places - fixed + offset_by * (used - fixed)) % max(1, amount - fixed)
        return jnp.zeros((amount,), jnp.int32).at[sequence[jnp.where(places < fixed, places, passed)]].set(jnp.asarray(tallies, jnp.int32))

    tallies = jnp.where(number % 4 == 0, named(packed, number // 4), named(usual, number - number // 4 - 1))
    mixed = jax.random.permutation(jax.random.fold_in(own, 3), amount)
    source_of, receiver = mixed[0:amount // 2 * 2:2], mixed[1:amount // 2 * 2:2]
    slack = jnp.minimum(tallies[source_of] - 1, most - tallies[receiver]) // 2
    slack = jnp.where((source_of == sequence[0]) | (receiver == sequence[0]) | (tallies[receiver] == 0), 0, jnp.maximum(slack, 0))
    passed = jax.random.randint(jax.random.fold_in(own, 4), (amount // 2,), 0, 1 << 20) % (slack + 1)
    tallies = tallies.at[source_of].add(-passed).at[receiver].add(passed)
    items = jnp.searchsorted(jnp.cumsum(tallies), jnp.arange(rows * top), side="right").astype(jnp.int32)
    table = items.reshape(top, rows).T
    table = table[jax.random.permutation(jax.random.fold_in(own, 1), rows)]
    offset_by = jax.random.randint(jax.random.fold_in(own, 2), (rows, 1), 0, top)
    return jnp.take_along_axis(table, (jnp.arange(top)[None, :] + offset_by) % top, axis=1)


def portions_of(number_of, total, most, slope, full):
    weights = [(1 << 20) // math.isqrt(grade ** slope) + 1 for grade in range(1, number_of + 1)]
    largest = most if full else min(most, max(-(-total // number_of), total * weights[0] // sum(weights)))
    least = 1 if total - largest >= number_of - 1 else 0
    given, rest = [largest] + [least] * (number_of - 1), total - largest - least * (number_of - 1)
    while rest > 0:
        free = [i for i in range(1, number_of) if given[i] < largest] or [i for i in range(1, number_of) if given[i] < most]
        pool, budget = sum([weights[i] for i in free]), rest
        for i in free:
            more = min(most - given[i], max(1, budget * weights[i] // pool), rest)
            given[i] = given[i] + more
            rest = rest - more
    return np.array(given)


def scatter_about(stream_key, dims, width, most, pieces=(), kind=jnp.bfloat16):
    result = jax.random.normal(stream_key, dims, jnp.float32) * width
    if len(pieces) > 0:
        result = levels(stream_key, dims, pieces, -0.22, 0.18) * result
    return jnp.clip(result, min=-most, max=most).astype(kind)


def setup_inputs(seed: int = 0) -> dict:
    arg_keys = jax.random.split(jax.random.key(seed), 12)
    queries = draw_queries(jax.random.fold_in(arg_keys[11], 71), 0)
    keys = draw_keys(jax.random.fold_in(arg_keys[11], 71), 0)
    values = scatter_about(arg_keys[2], (TOKENS, HEADS * HEAD_DIM), 1.0, 6.0, ((0, 8), (1, 4)))
    lengths = ragged_sizes(arg_keys[3], TENANTS, TOKENS, TOKENS // 2, 2).astype(jnp.int32)
    resid = scatter_about(arg_keys[4], (TOKENS, D), 0.5, 6.0, ((0, 32),))
    w_out = scatter_about(arg_keys[5], (HEADS * HEAD_DIM, D), HEAD_DIM ** -0.5, 0.5, ((0, 4),))
    moe_gain = jnp.clip(1.0 + 0.15 * jax.random.normal(arg_keys[6], (D,), jnp.float32), 0.25, 1.75)
    routes_keys = jax.random.split(jax.random.fold_in(arg_keys[7], 1), TOKENS // ROWS_DEV)
    routes_turns = jax.random.permutation(jax.random.fold_in(arg_keys[7], 3), TOKENS // ROWS_DEV)
    routes = jax.vmap(lambda own, number: assign_block(jax.random.fold_in(arg_keys[7], 2), own, number, ROWS_DEV, EXPERTS, TOP, CAP, 2))(routes_keys, routes_turns).reshape((TOKENS, TOP))
    gates = jnp.clip(0.05 + 0.25 * jax.random.uniform(arg_keys[8], (TOKENS, TOP), jnp.float32) ** levels(arg_keys[8], (TOKENS, TOP), ((0, 32),), -0.2, 0.2), 0.05, 0.3)
    w_gate_up = scatter_about(arg_keys[9], (EXPERTS, D, 2, FF), D ** -0.5, 0.125, ((0, 8), (3, 4)))
    w_down = scatter_about(arg_keys[10], (EXPERTS, FF, D), FF ** -0.5, 0.1875, ((0, 8), (1, 4)))
    return dict(queries=queries, keys=keys, values=values, lengths=lengths, resid=resid, w_out=w_out, moe_gain=moe_gain, routes=routes, gates=gates, w_gate_up=w_gate_up, w_down=w_down)


def tenant_of(positions, lengths):
    bounds = jnp.cumsum(lengths).astype(jnp.int32)
    return lax.optimization_barrier(jnp.sum((positions[:, None] >= bounds[None, :]).astype(jnp.int32), axis=1))

def reference(queries, keys, values, lengths, resid, w_out, moe_gain, routes, gates, w_gate_up, w_down):
    positions = jnp.arange(TOKENS, dtype=jnp.int32)
    tenant = tenant_of(positions, lengths)
    visible = (tenant[:, None] == tenant[None, :]) & (positions[None, :] <= positions[:, None])
    score_scale = 1.0 / math.sqrt(HEAD_DIM)
    q_heads = queries.reshape(TOKENS, HEADS, HEAD_DIM).transpose(1, 0, 2)
    k_heads = keys.reshape(TOKENS, HEADS, HEAD_DIM).transpose(1, 0, 2)
    v_heads = values.reshape(TOKENS, HEADS, HEAD_DIM).transpose(1, 0, 2)

    def one_head(operands):
        q_block, k_block, v_block = operands
        scores = jnp.dot(q_block, k_block.T, preferred_element_type=jnp.float32) * score_scale
        scores = jnp.where(visible, scores, -jnp.inf)
        largest = lax.optimization_barrier(jnp.max(scores, axis=1, keepdims=True))
        weights = jnp.where(visible, jnp.exp(scores - largest), 0.0)
        denominator = lax.optimization_barrier(jnp.sum(weights, axis=1, keepdims=True))
        rounded_weights = weights.astype(jnp.bfloat16)
        weighted = jnp.dot(rounded_weights, v_block, preferred_element_type=jnp.float32)
        return (weighted / denominator).astype(jnp.bfloat16)
    heads_out = lax.map(one_head, (q_heads, k_heads, v_heads))
    attention = heads_out.transpose(1, 0, 2).reshape(TOKENS, HEADS * HEAD_DIM)
    projected = jnp.dot(attention, w_out, preferred_element_type=jnp.float32)
    attended = (resid.astype(jnp.float32) + projected).astype(jnp.bfloat16)
    widened = attended.astype(jnp.float32)
    meansq = lax.optimization_barrier(jnp.mean(widened * widened, axis=1, keepdims=True))
    normed = (widened * lax.rsqrt(meansq + 1e-05) * moe_gain[None, :]).astype(jnp.bfloat16)
    ff_part = FF // N_TP
    max_rows = CAP * (TOKENS // ROWS_DEV)
    expert_ids = jnp.arange(EXPERTS, dtype=jnp.int32)
    matches = routes[:, :, None] == expert_ids[None, None, :]
    weight_of = lax.optimization_barrier(jnp.sum(jnp.where(matches, gates[:, :, None], 0.0), axis=1))
    members = jnp.any(matches, axis=1)

    def per_expert(summed, expert):
        column = lax.dynamic_index_in_dim(members, expert, 1, keepdims=False)
        how_many = jnp.sum(column.astype(jnp.int32))
        chosen_rows = jnp.nonzero(column, size=max_rows, fill_value=0)[0].astype(jnp.int32)
        selected = normed[chosen_rows]
        gate_up = w_gate_up[expert]
        gate_proj = jnp.dot(selected, gate_up[:, 0, :], preferred_element_type=jnp.float32)
        up_proj = jnp.dot(selected, gate_up[:, 1, :], preferred_element_type=jnp.float32)
        hidden = (jax.nn.silu(gate_proj) * up_proj).astype(jnp.bfloat16)
        down_rows = w_down[expert]
        blocks_total = jnp.zeros((max_rows, D), jnp.float32)
        for block_index in range(N_TP):
            partial_value = jnp.dot(hidden[:, block_index * ff_part:(block_index + 1) * ff_part], down_rows[block_index * ff_part:(block_index + 1) * ff_part], preferred_element_type=jnp.float32)
            blocks_total = blocks_total + lax.optimization_barrier(partial_value.astype(jnp.bfloat16)).astype(jnp.float32)
        expert_out = lax.optimization_barrier(blocks_total.astype(jnp.bfloat16)).astype(jnp.float32)
        in_use = jnp.arange(max_rows, dtype=jnp.int32) < how_many
        factor = jnp.where(in_use, weight_of[chosen_rows, expert], 0.0)
        summed = summed.at[chosen_rows].add(factor[:, None] * expert_out)
        return (summed, None)
    mixed_total, _ = lax.scan(per_expert, jnp.zeros((TOKENS, D), jnp.float32), expert_ids)
    expert_mix = mixed_total.astype(jnp.bfloat16)
    return (attended, expert_mix)
```

```python
import functools
import math

import jax
import jax.numpy as jnp
from jax import lax
from jax.experimental import pallas as pl
from jax.experimental.pallas import tpu as pltpu
from jax.sharding import PartitionSpec as P

HEAD_DIM = 128
F32 = jnp.float32
BF16 = jnp.bfloat16


def over_y(a):
    count = lax.axis_size("seq")
    return lax.ppermute(a, "seq", [(i, i ^ 1) for i in range(count)])


def over_z(a, step):
    count = lax.axis_size("seq")
    return lax.ppermute(a, "seq", [(i, (i + 2 * step) % count) for i in range(count)])


def over_x(a):
    return lax.ppermute(a, "tp", [(i, i ^ 2) for i in range(4)])


def over_core(a):
    return lax.ppermute(a, "tp", [(i, i ^ 1) for i in range(4)])


def ring_gather(unit, down_from=0):
    half = lax.axis_size("seq") // 4
    middle = unit.shape[0] // 2
    up, down = [unit], [unit[down_from:]]
    for _ in range(1, half):
        up.append(over_z(up[-1], 1))
        down.append(over_z(down[-1], -1))
    far = (over_z(up[-1][:middle], 1), over_z(down[-1][middle - down_from :], -1))
    return up, down, far


def ring_scatter(parts):
    half = lax.axis_size("seq") // 4
    middle = parts.shape[1] // 2
    own, ups, downs, far = parts[0], parts[1:half], parts[half:-1], parts[-1]
    plus = over_z(far[:middle], 1)
    minus = over_z(far[middle:], -1)
    for k in reversed(range(half - 1)):
        high, low = downs[k], ups[k]
        if plus.shape[0] == middle:
            high = jnp.concatenate([add(high[:middle], plus), high[middle:]], 0)
            low = jnp.concatenate([low[:middle], add(low[middle:], minus)], 0)
        else:
            high, low = add(high, plus), add(low, minus)
        plus, minus = over_z(high, 1), over_z(low, -1)
    return (own.astype(F32) + plus.astype(F32) + minus.astype(F32)).astype(BF16)


def add(a, b):
    return (a.astype(F32) + b.astype(F32)).astype(BF16)


def relative_rows(a, x, core):
    blocks = a.reshape((2, 2, a.shape[0] // 4) + a.shape[1:])
    blocks = jnp.where(x == 0, blocks, blocks[::-1])
    blocks = jnp.where(core == 0, blocks, blocks[:, ::-1])
    return jnp.swapaxes(blocks, 0, 1).reshape(a.shape)


def attention_kernel(scale, bases, q_ref, pos_ref, start_ref, *refs):
    kv_refs, out_ref = refs[:-1], refs[-1]
    piece = q_ref.shape[0] // 2
    key_pos, n = [], 0
    for kv in kv_refs:
        rows = kv.shape[0]
        column = lax.broadcasted_iota(jnp.int32, (1, rows), 1)
        if rows == piece:
            key_pos.append(column + bases[n])
            n += 1
        else:
            key_pos.append(
                jnp.where(column < piece, column + bases[n], column + (bases[n + 1] - piece))
            )
            n += 2
    width = q_ref.shape[1]
    for part in range(2):
        rows = pl.ds(part * piece, piece)
        pos, start = pos_ref[rows, :], start_ref[rows, :]
        masks = [(k >= start) & (k <= pos) for k in key_pos]
        for head in range(width // HEAD_DIM):
            lanes = pl.ds(head * HEAD_DIM, HEAD_DIM)
            value_lanes = pl.ds(width + head * HEAD_DIM, HEAD_DIM)
            q = q_ref[rows, lanes]
            scores = [
                jnp.where(
                    mask,
                    lax.dot_general(
                        q, kv[:, lanes], (((1,), (1,)), ((), ())), preferred_element_type=F32
                    )
                    * scale,
                    -1e30,
                )
                for kv, mask in zip(kv_refs, masks)
            ]
            top = functools.reduce(jnp.maximum, [jnp.max(v, axis=1, keepdims=True) for v in scores])
            total, mixed = 0.0, 0.0
            for kv, mask, score in zip(kv_refs, masks, scores):
                weight = jnp.where(mask, jnp.exp(score - top), 0.0)
                total = total + jnp.sum(weight, axis=1, keepdims=True)
                mixed = mixed + jnp.dot(
                    weight.astype(BF16), kv[:, value_lanes], preferred_element_type=F32
                )
            out_ref[rows, lanes] = (mixed / total).astype(BF16)


def attend(q, pos, start, bases, blocks):
    vmem = pl.BlockSpec(memory_space=pltpu.VMEM)
    keys = sum(b.shape[0] for b in blocks)
    return pl.pallas_call(
        functools.partial(attention_kernel, 1.0 / math.sqrt(HEAD_DIM)),
        out_shape=jax.ShapeDtypeStruct(q.shape, BF16),
        in_specs=[pl.BlockSpec(memory_space=pltpu.SMEM)] + [vmem] * (3 + len(blocks)),
        out_specs=vmem,
        compiler_params=pltpu.CompilerParams(vmem_limit_bytes=40 * 1024 * 1024),
        cost_estimate=pl.CostEstimate(
            flops=4 * q.shape[0] * q.shape[1] * keys,
            bytes_accessed=4 * q.size + 4 * keys * q.shape[1],
            transcendentals=q.shape[0] * q.shape[1] // HEAD_DIM * keys,
        ),
    )(bases, q, pos, start, *blocks)


def attention(queries, keys, values, lengths, seq, x, core):
    ring = lax.axis_size("seq") // 2
    y, z = seq % 2, seq // 2
    rows, width = queries.shape
    half = width // 2

    def split(a):
        left, right = a[:, :half], a[:, half:]
        return jnp.where(y == 0, left, right), jnp.where(y == 0, right, left)

    (k_own, k_other), (v_own, v_other) = split(keys), split(values)
    kv = jnp.concatenate([k_own, v_own], 1)
    kv_other = over_y(jnp.concatenate([k_other, v_other], 1))
    q_own, q_other = split(relative_rows(queries, x, core))
    q = jnp.concatenate([q_own, over_y(q_other)], 0)
    up, _, far = ring_gather(jnp.concatenate([kv, kv_other], 0), rows)
    blocks = list(up) + list(far)
    shard = [((z - k) % ring) * 2 + other for k in range(ring // 2 + 1) for other in (y, 1 - y)]
    bases = jnp.stack(shard).astype(jnp.int32) * rows

    local = relative_rows(jnp.arange(rows, dtype=jnp.int32), x, core)
    pos = jnp.concatenate([seq * rows + local, (seq ^ 1) * rows + local])
    bounds = jnp.cumsum(lengths)
    start = jnp.max(jnp.where(bounds[None, :] <= pos[:, None], bounds[None, :], 0), axis=1)
    out = attend(q, pos[:, None], start[:, None], bases, blocks)
    return out[:rows], over_y(out[rows:])


def gather_tokens(unit):
    middle = unit.shape[0] // 2
    up, down, far = ring_gather(unit)
    beside = over_y(unit)
    r_up, r_down, r_far = ring_gather(beside[middle:])
    pieces = [unit, beside]
    for own, right in zip(up[1:] + down[1:], r_up[1:] + r_down[1:]):
        pieces += [own, over_y(own[:middle]), right]
    pieces += [far[0], far[1], over_y(far[0]), r_far[0], r_far[1]]
    return jnp.concatenate(pieces, 0)


def experts(tokens, width, first, w_in, w_down):
    owned = w_down.shape[0]
    inner = w_down.shape[1]
    count = lax.axis_size("seq") * owned
    weight = tokens[:, width : width + count].astype(F32)
    weight = weight + tokens[:, width + count : width + 2 * count].astype(F32)
    column = lax.broadcasted_iota(jnp.int32, (1, count), 1)
    projections = jnp.dot(tokens[:, :width], w_in, preferred_element_type=F32)
    hidden = []
    for e in range(owned):
        factor = jnp.sum(jnp.where(column == first + e, weight, 0.0), axis=1, keepdims=True)
        gate = projections[:, 2 * e * inner : (2 * e + 1) * inner]
        up = projections[:, (2 * e + 1) * inner : (2 * e + 2) * inner]
        hidden.append(jnp.where(factor > 0, jax.nn.silu(gate) * up * factor, 0.0).astype(BF16))
    return jnp.dot(
        jnp.concatenate(hidden, 1),
        w_down.reshape(owned * inner, width),
        preferred_element_type=F32,
    )


def scatter_sums(total, rows):
    width = total.shape[1]
    ring = lax.axis_size("seq") // 2
    first = width * 5 // 16
    total = total.reshape(ring, 2, 2, rows, width)
    a, b, c = total[..., :first], total[..., first : 2 * first], total[..., 2 * first :]
    a = add(a[:, :, 0], over_x(a[:, :, 1]))
    b = add(b[:, 0], over_y(b[:, 1]))
    c = ring_scatter(c.reshape(ring, 4 * rows, -1)).reshape(2, 2 * rows, -1)
    ab = ring_scatter(jnp.concatenate([a, b], 1).reshape(ring, 4 * rows, -1))
    ab = ab.reshape(4, rows, -1)
    c = add(c[0], over_y(c[1])).reshape(2, rows, -1)
    a = add(ab[0], over_y(ab[1]))
    b = add(ab[2], over_x(ab[3]))
    c = add(c[0], over_x(c[1]))
    return jnp.concatenate([a, b, c], 1)


def shards(
    queries, keys, values, lengths, resid, w_out, moe_gain, routes, gates, w_gate_up, w_down
):
    seq, tp = lax.axis_index("seq"), lax.axis_index("tp")
    x, core, y = tp // 2, tp % 2, seq % 2
    rows, width = resid.shape
    owned = w_gate_up.shape[0]
    count = owned * lax.axis_size("seq")
    half = w_out.shape[0] // 2

    own, other = attention(queries, keys, values, lengths, seq, x, core)
    w_own = jnp.where(y == 0, w_out[:half], w_out[half:])
    w_other = jnp.where(y == 0, w_out[half:], w_out[:half])
    projected = jnp.dot(own, w_own, preferred_element_type=F32)
    projected = projected + jnp.dot(other, w_other, preferred_element_type=F32)

    matches = routes[:, :, None] == jnp.arange(count, dtype=jnp.int32)[None, None, :]
    weight = jnp.sum(jnp.where(matches, gates[:, :, None], 0.0), axis=1)
    high = weight.astype(BF16)
    low = (weight - high.astype(F32)).astype(BF16)
    pad = -(-2 * count // 128) * 128 - 2 * count
    packed = jnp.concatenate([high, low, jnp.zeros((rows, pad), BF16)], 1)
    packed = jnp.concatenate([packed, over_x(packed)], 0)

    received = over_core(projected[2 * rows :].astype(BF16))
    partial = projected[: 2 * rows] + received.astype(F32)
    partial = jnp.concatenate([partial[:rows] + resid.astype(F32), partial[rows:]], 0)
    arrived = over_x(partial.astype(BF16)).reshape(2, rows, width)[::-1]
    attended = (partial + arrived.reshape(2 * rows, width).astype(F32)).astype(BF16)
    widened = attended.astype(F32)
    meansq = jnp.mean(widened * widened, axis=1, keepdims=True)
    normed = (widened * lax.rsqrt(meansq + 1e-05) * moe_gain[None, :]).astype(BF16)

    tokens = gather_tokens(jnp.concatenate([normed, packed], 1))
    tokens_other = over_core(tokens)
    w_in = w_gate_up.transpose(1, 0, 2, 3).reshape(width, -1)
    first = owned * seq
    sums_other = experts(tokens_other, width, first, w_in, w_down).astype(BF16)
    sums = experts(tokens, width, first, w_in, w_down)
    sums = (sums + over_core(sums_other).astype(F32)).astype(BF16)
    return attended[:rows], scatter_sums(sums, rows)


def solution(mesh):
    return jax.shard_map(
        shards,
        mesh=mesh,
        in_specs=(
            P("seq", "tp"),
            P("seq", "tp"),
            P("seq", "tp"),
            P(),
            P(("seq", "tp"), None),
            P("tp", None),
            P(),
            P(("seq", "tp"), None),
            P(("seq", "tp"), None),
            P("seq", None, None, "tp"),
            P("seq", "tp", None),
        ),
        out_specs=(P(("seq", "tp"), None), P(("seq", "tp"), None)),
        check_vma=False,
    )
```

```python
import functools
import math

import jax
import jax.numpy as jnp
from jax import lax
from jax.experimental import pallas as pl
from jax.experimental.pallas import tpu as pltpu
from jax.sharding import PartitionSpec as P

HEAD_DIM = 128
F32 = jnp.float32
BF16 = jnp.bfloat16


def over_y(a):
    count = lax.axis_size("seq")
    return lax.ppermute(a, "seq", [(i, i ^ 1) for i in range(count)])


def over_z(a, step):
    count = lax.axis_size("seq")
    return lax.ppermute(a, "seq", [(i, (i + 2 * step) % count) for i in range(count)])


def over_x(a):
    return lax.ppermute(a, "tp", [(i, i ^ 2) for i in range(4)])


def over_core(a):
    return lax.ppermute(a, "tp", [(i, i ^ 1) for i in range(4)])


def add(a, b):
    return (a.astype(F32) + b.astype(F32)).astype(BF16)


def relative_rows(a, x, core):
    blocks = a.reshape((2, 2, a.shape[0] // 4) + a.shape[1:])
    blocks = jnp.where(x == 0, blocks, blocks[::-1])
    blocks = jnp.where(core == 0, blocks, blocks[:, ::-1])
    return jnp.swapaxes(blocks, 0, 1).reshape(a.shape)


def attention_kernel(scale, bases, q_ref, pos_ref, start_ref, *refs):
    kv_refs, out_ref = refs[:-1], refs[-1]
    piece = q_ref.shape[0] // 2
    key_pos, n = [], 0
    for kv in kv_refs:
        rows = kv.shape[0]
        column = lax.broadcasted_iota(jnp.int32, (1, rows), 1)
        if rows == piece:
            key_pos.append(column + bases[n])
            n += 1
        else:
            key_pos.append(
                jnp.where(column < piece, column + bases[n], column + (bases[n + 1] - piece))
            )
            n += 2
    width = q_ref.shape[1]
    for part in range(2):
        rows = pl.ds(part * piece, piece)
        pos, start = pos_ref[rows, :], start_ref[rows, :]
        masks = [(k >= start) & (k <= pos) for k in key_pos]
        for head in range(width // HEAD_DIM):
            lanes = pl.ds(head * HEAD_DIM, HEAD_DIM)
            value_lanes = pl.ds(width + head * HEAD_DIM, HEAD_DIM)
            q = q_ref[rows, lanes]
            scores = [
                jnp.where(
                    mask,
                    lax.dot_general(
                        q, kv[:, lanes], (((1,), (1,)), ((), ())), preferred_element_type=F32
                    )
                    * scale,
                    -1e30,
                )
                for kv, mask in zip(kv_refs, masks)
            ]
            top = functools.reduce(jnp.maximum, [jnp.max(v, axis=1, keepdims=True) for v in scores])
            total, mixed = 0.0, 0.0
            for kv, mask, score in zip(kv_refs, masks, scores):
                weight = jnp.where(mask, jnp.exp(score - top), 0.0)
                total = total + jnp.sum(weight, axis=1, keepdims=True)
                mixed = mixed + jnp.dot(
                    weight.astype(BF16), kv[:, value_lanes], preferred_element_type=F32
                )
            out_ref[rows, lanes] = (mixed / total).astype(BF16)


def attend(q, pos, start, bases, blocks):
    vmem = pl.BlockSpec(memory_space=pltpu.VMEM)
    keys = sum(b.shape[0] for b in blocks)
    return pl.pallas_call(
        functools.partial(attention_kernel, 1.0 / math.sqrt(HEAD_DIM)),
        out_shape=jax.ShapeDtypeStruct(q.shape, BF16),
        in_specs=[pl.BlockSpec(memory_space=pltpu.SMEM)] + [vmem] * (3 + len(blocks)),
        out_specs=vmem,
        compiler_params=pltpu.CompilerParams(vmem_limit_bytes=40 * 1024 * 1024),
        cost_estimate=pl.CostEstimate(
            flops=4 * q.shape[0] * q.shape[1] * keys,
            bytes_accessed=4 * q.size + 4 * keys * q.shape[1],
            transcendentals=q.shape[0] * q.shape[1] // HEAD_DIM * keys,
        ),
    )(bases, q, pos, start, *blocks)


def attention(queries, keys, values, lengths, seq, x, core, w_in, w_down):
    ring = lax.axis_size("seq") // 2
    y, z = seq % 2, seq // 2
    rows, width = queries.shape
    half = width // 2

    def split(a):
        left, right = a[:, :half], a[:, half:]
        return jnp.where(y == 0, left, right), jnp.where(y == 0, right, left)

    (k_own, k_other), (v_own, v_other) = split(keys), split(values)
    own, beside = jnp.concatenate([k_own, v_own], 1), jnp.concatenate([k_other, v_other], 1)
    own, beside, queries, w_in, w_down = lax.optimization_barrier(
        (own, beside, queries, w_in, w_down)
    )
    q_own, q_other = split(relative_rows(queries, x, core))
    beside = over_y(beside)
    blocks, shard = [own, beside], [2 * z + y, 2 * z + 1 - y]
    q = jnp.concatenate([q_own, over_y(q_other)], 0)
    w_in = lax.optimization_barrier(w_in.transpose(0, 2, 1, 3))
    weights = (w_in, over_core(w_in)), (w_down, over_core(w_down))
    for k in range(1, ring // 2 + 1):
        own = over_z(own, 1)
        if k == 1:
            own, beside = lax.optimization_barrier((own, beside))
        beside = over_z(beside, 1)
        blocks += [own, beside]
        shard += [2 * (z - k) + y, 2 * (z - k) + 1 - y]
    bases = jnp.stack(shard).astype(jnp.int32) * rows

    local = relative_rows(jnp.arange(rows, dtype=jnp.int32), x, core)
    pos = jnp.concatenate([seq * rows + local, (seq ^ 1) * rows + local])
    bounds = jnp.cumsum(lengths)
    start = jnp.max(jnp.where(bounds[None, :] <= pos[:, None], bounds[None, :], 0), axis=1)
    blocks, weights = lax.optimization_barrier((blocks, weights))
    out = attend(q, pos[:, None], start[:, None], bases, blocks)
    return out[:rows], over_y(out[rows:]), weights


def expert_kernel(
    count,
    first,
    a,
    b,
    y_a,
    x_b,
    x_aa,
    y_bb,
    in_own,
    in_other,
    down_own,
    down_other,
    a_keep,
    a_send,
    b_keep,
    b_send,
    tokens,
    factors,
    total,
):
    step = pl.program_id(0)
    owned = pl.num_programs(0) // 2
    groups, rows, half = a.shape

    @pl.when(step == 0)
    def _():
        column = lax.broadcasted_iota(jnp.int32, (1, count), 1)
        for g in range(groups):
            quarters = (
                (a.at[g], b.at[g]),
                (x_aa.at[g, 0], x_b.at[g]),
                (y_a.at[g], y_bb.at[g, 0]),
                (x_aa.at[g, 1], y_bb.at[g, 1]),
            )
            for i, (left, right) in enumerate(quarters):
                at = pl.ds((4 * g + i) * rows, rows)
                tokens[at, :half] = left[...]
                tokens[at, half:] = right[:, :half]
                packed = right[:, half:].astype(F32)
                weight = packed[:, :count] + packed[:, count : 2 * count]
                for e in range(factors.shape[0]):
                    chosen = jnp.where(column == first[0] + e, weight, 0.0)
                    factor = jnp.sum(chosen, axis=1, keepdims=True)
                    factors[e, at, :] = jnp.broadcast_to(factor, (rows, factors.shape[2]))

    def expert(w_in, w_down):
        gate = jnp.dot(tokens[...], w_in[0, 0], preferred_element_type=F32)
        up = jnp.dot(tokens[...], w_in[0, 1], preferred_element_type=F32)
        factor = factors[lax.rem(step, owned)][:, :1]
        hidden = jnp.where(factor > 0, gate / (1.0 + jnp.exp(-gate)) * up * factor, 0.0)
        return jnp.dot(hidden.astype(BF16), w_down[0], preferred_element_type=F32)

    @pl.when(step == 0)
    def _():
        total[...] = expert(in_own, down_own)

    @pl.when((step > 0) & (step < owned))
    def _():
        total[...] += expert(in_own, down_own)

    @pl.when(step >= owned)
    def _():
        total[...] += expert(in_other, down_other)

    @pl.when(step == 2 * owned - 1)
    def _():
        for g in range(groups):
            for i in range(4):
                at = pl.ds((4 * g + i) * rows, rows)
                y, x = divmod(i, 2)
                (a_send if x else a_keep)[g, y] = total[at, :half].astype(BF16)
                (b_send if y else b_keep)[g, x] = total[at, half:].astype(BF16)


def experts(first, count, pieces, weights):
    (in_own, in_other), (down_own, down_other) = weights
    groups, rows, half = pieces[0].shape
    owned, _, width, inner = in_own.shape
    n = groups * 4 * rows

    def whole(a):
        return pl.BlockSpec(a.shape, lambda i, zeros=(0,) * a.ndim: zeros)

    def early(i):
        return jnp.minimum(i, owned - 1)

    def late(i):
        return jnp.maximum(i - owned, 0)

    out = jax.ShapeDtypeStruct((groups, 2, rows, half), BF16)
    in_block, down_block = (1, 2, width, inner), (1, inner, width)
    return pl.pallas_call(
        functools.partial(expert_kernel, count),
        grid=(2 * owned,),
        out_shape=[out] * 4,
        in_specs=[pl.BlockSpec(memory_space=pltpu.SMEM)]
        + [whole(a) for a in pieces]
        + [
            pl.BlockSpec(in_block, lambda i: (early(i), 0, 0, 0)),
            pl.BlockSpec(in_block, lambda i: (late(i), 0, 0, 0)),
            pl.BlockSpec(down_block, lambda i: (early(i), 0, 0)),
            pl.BlockSpec(down_block, lambda i: (late(i), 0, 0)),
        ],
        out_specs=[whole(out)] * 4,
        scratch_shapes=[
            pltpu.VMEM((n, width), BF16),
            pltpu.VMEM((owned, n, 128), F32),
            pltpu.VMEM((n, width), F32),
        ],
        compiler_params=pltpu.CompilerParams(vmem_limit_bytes=40 * 1024 * 1024),
        cost_estimate=pl.CostEstimate(
            flops=12 * n * owned * width * inner,
            bytes_accessed=12 * owned * width * inner + 4 * n * width,
            transcendentals=2 * n * owned * inner,
        ),
    )(first, *pieces, in_own, in_other, down_own, down_other)


def plane_first(unit):
    half = (unit.shape[2] - 128) // 2
    a, b = unit[..., :half], unit[..., half:]
    return a, b, over_y(a), over_x(b)


def plane_second(a, b, y_a, x_b):
    return a, b, y_a, x_b, over_x(jnp.stack([a, y_a], 1)), over_y(jnp.stack([b, x_b], 1))


def gather_tokens(unit, use):
    half = lax.axis_size("seq") // 4
    middle = (unit.shape[1] - 128) // 2
    own_first = plane_first(unit[None])
    up, down, pairs = unit, unit, []
    for _ in range(1, half):
        up, down = over_z(up, 1), over_z(down, -1)
        pairs.append(jnp.stack([up, down]))
    far_a, far_b = over_z(up[:, :middle], 1)[None], over_z(down[:, middle:], -1)[None]
    used = use(plane_second(*own_first))
    done = [used]
    for pair in pairs:
        first = plane_first(pair)
        first, done[-1] = lax.optimization_barrier((first, done[-1]))
        done.append(use(plane_second(*first)))
    first = far_a, far_b, over_y(far_a), over_x(far_b)
    first, done[-1] = lax.optimization_barrier((first, done[-1]))
    return done[0], use(plane_second(*first)), done[1:]


def plane_scatter(a_keep, a_send, b_keep, b_send):
    a = add(a_keep, over_x(a_send))
    b = add(b_keep, over_y(b_send))
    return add(a[:, 0], over_y(a[:, 1])), add(b[:, 0], over_x(b[:, 1]))


def ring_scatter(own, far, pairs):
    (far_a, far_b) = far
    plus, minus = over_z(far_a[0], 1), over_z(far_b[0], -1)
    last = len(pairs) - 1
    for k in reversed(range(last + 1)):
        a, b = pairs[k]
        if k == last:
            high = jnp.concatenate([add(a[1], plus), b[1]], 1)
            low = jnp.concatenate([a[0], add(b[0], minus)], 1)
        else:
            high = add(jnp.concatenate([a[1], b[1]], 1), plus)
            low = add(jnp.concatenate([a[0], b[0]], 1), minus)
        plus, minus = over_z(high, 1), over_z(low, -1)
    own = jnp.concatenate([own[0][0], own[1][0]], 1)
    return (own.astype(F32) + plus.astype(F32) + minus.astype(F32)).astype(BF16)


def shards(
    queries, keys, values, lengths, resid, w_out, moe_gain, routes, gates, w_gate_up, w_down
):
    seq, tp = lax.axis_index("seq"), lax.axis_index("tp")
    x, core, y = tp // 2, tp % 2, seq % 2
    rows = resid.shape[0]
    owned = w_gate_up.shape[0]
    count = owned * lax.axis_size("seq")
    half = w_out.shape[0] // 2

    own, other, weights = attention(
        queries, keys, values, lengths, seq, x, core, w_gate_up, w_down
    )
    w_own = jnp.where(y == 0, w_out[:half], w_out[half:])
    w_other = jnp.where(y == 0, w_out[half:], w_out[:half])
    projected = jnp.dot(own, w_own, preferred_element_type=F32)
    projected = projected + jnp.dot(other, w_other, preferred_element_type=F32)

    matches = routes[:, :, None] == jnp.arange(count, dtype=jnp.int32)[None, None, :]
    weight = jnp.sum(jnp.where(matches, gates[:, :, None], 0.0), axis=1)
    high = weight.astype(BF16)
    low = (weight - high.astype(F32)).astype(BF16)
    pad = -(-2 * count // 128) * 128 - 2 * count
    packed = jnp.concatenate([high, low, jnp.zeros((rows, pad), BF16)], 1)

    received = over_core(projected[2 * rows :].astype(BF16))
    partial = projected[: 2 * rows] + received.astype(F32)
    arrived = over_x(partial[rows:].astype(BF16))
    attended = (resid.astype(F32) + partial[:rows] + arrived.astype(F32)).astype(BF16)
    widened = attended.astype(F32)
    meansq = jnp.mean(widened * widened, axis=1, keepdims=True)
    normed = (widened * lax.rsqrt(meansq + 1e-05) * moe_gain[None, :]).astype(BF16)

    first = (owned * seq).astype(jnp.int32).reshape(1)
    own, far, pairs = gather_tokens(
        jnp.concatenate([normed, packed], 1),
        lambda pieces: experts(first, count, pieces, weights),
    )
    far = plane_scatter(*far)
    pairs = [plane_scatter(*pair) for pair in pairs]
    return attended, ring_scatter(plane_scatter(*own), far, pairs)


def solution(mesh):
    return jax.shard_map(
        shards,
        mesh=mesh,
        in_specs=(
            P("seq", "tp"),
            P("seq", "tp"),
            P("seq", "tp"),
            P(),
            P(("seq", "tp"), None),
            P("tp", None),
            P(),
            P(("seq", "tp"), None),
            P(("seq", "tp"), None),
            P("seq", None, None, "tp"),
            P("seq", "tp", None),
        ),
        out_specs=(P(("seq", "tp"), None), P(("seq", "tp"), None)),
        check_vma=False,
    )
```

```python
import functools
import math

import jax
import jax.numpy as jnp
from jax import lax
from jax.experimental import pallas as pl
from jax.experimental.pallas import tpu as pltpu
from jax.sharding import PartitionSpec as P

HEAD_DIM = 128
F32 = jnp.float32
BF16 = jnp.bfloat16
VMEM_LIMIT = 20 * 1024 * 1024


def over_y(a):
    count = lax.axis_size("seq")
    return lax.ppermute(a, "seq", [(i, i ^ 1) for i in range(count)])


def over_z(a, step):
    count = lax.axis_size("seq")
    return lax.ppermute(a, "seq", [(i, (i + 2 * step) % count) for i in range(count)])


def over_x(a):
    return lax.ppermute(a, "tp", [(i, i ^ 2) for i in range(4)])


def over_core(a):
    return lax.ppermute(a, "tp", [(i, i ^ 1) for i in range(4)])


def add(a, b):
    return (a.astype(F32) + b.astype(F32)).astype(BF16)


def relative_rows(a, x, core):
    blocks = a.reshape((2, 2, a.shape[0] // 4) + a.shape[1:])
    blocks = jnp.where(x == 0, blocks, blocks[::-1])
    blocks = jnp.where(core == 0, blocks, blocks[:, ::-1])
    return jnp.swapaxes(blocks, 0, 1).reshape(a.shape)


def attention_kernel(scale, bases, q_own, q_beside, pos_ref, start_ref, *refs):
    kv_refs, out_ref = refs[:-1], refs[-1]
    piece, width = q_own.shape
    key_pos, n = [], 0
    for kv in kv_refs:
        rows = kv.shape[0]
        column = lax.broadcasted_iota(jnp.int32, (1, rows), 1)
        if rows == piece:
            key_pos.append(column + bases[n])
            n += 1
        else:
            key_pos.append(
                jnp.where(column < piece, column + bases[n], column + (bases[n + 1] - piece))
            )
            n += 2
    for part, q_ref in enumerate((q_own, q_beside)):
        rows = pl.ds(part * piece, piece)
        pos, start = pos_ref[rows, :], start_ref[rows, :]
        masks = [(k >= start) & (k <= pos) for k in key_pos]
        for head in range(width // HEAD_DIM):
            lanes = pl.ds(head * HEAD_DIM, HEAD_DIM)
            value_lanes = pl.ds(width + head * HEAD_DIM, HEAD_DIM)
            q = q_ref[:, lanes]
            scores = [
                jnp.where(
                    mask,
                    lax.dot_general(
                        q, kv[:, lanes], (((1,), (1,)), ((), ())), preferred_element_type=F32
                    )
                    * scale,
                    -1e30,
                )
                for kv, mask in zip(kv_refs, masks)
            ]
            top = functools.reduce(jnp.maximum, [jnp.max(v, axis=1, keepdims=True) for v in scores])
            total, mixed = 0.0, 0.0
            for kv, mask, score in zip(kv_refs, masks, scores):
                weight = jnp.where(mask, jnp.exp(score - top), 0.0)
                total = total + jnp.sum(weight, axis=1, keepdims=True)
                mixed = mixed + jnp.dot(
                    weight.astype(BF16), kv[:, value_lanes], preferred_element_type=F32
                )
            out_ref[rows, lanes] = (mixed / total).astype(BF16)


def attend(q, beside, pos, start, bases, blocks):
    vmem = pl.BlockSpec(memory_space=pltpu.VMEM)
    keys = sum(b.shape[0] for b in blocks)
    return pl.pallas_call(
        functools.partial(attention_kernel, 1.0 / math.sqrt(HEAD_DIM)),
        out_shape=jax.ShapeDtypeStruct((2 * q.shape[0], q.shape[1]), BF16),
        in_specs=[pl.BlockSpec(memory_space=pltpu.SMEM)] + [vmem] * (4 + len(blocks)),
        out_specs=vmem,
        compiler_params=pltpu.CompilerParams(vmem_limit_bytes=VMEM_LIMIT),
        cost_estimate=pl.CostEstimate(
            flops=8 * q.size * keys,
            bytes_accessed=8 * q.size + 4 * keys * q.shape[1],
            transcendentals=2 * q.size // HEAD_DIM * keys,
        ),
    )(bases, q, beside, pos, start, *blocks)


def attention(queries, keys, values, lengths, seq, x, core, w_in, w_down):
    ring = lax.axis_size("seq") // 2
    y, z = seq % 2, seq // 2
    rows, width = queries.shape
    half = width // 2

    def split(a):
        left, right = a[:, :half], a[:, half:]
        return jnp.where(y == 0, left, right), jnp.where(y == 0, right, left)

    (k_own, k_other), (v_own, v_other) = split(keys), split(values)
    own, beside = jnp.concatenate([k_own, v_own], 1), jnp.concatenate([k_other, v_other], 1)
    own, beside, queries = lax.optimization_barrier((own, beside, queries))
    q_own, q_other = split(relative_rows(queries, x, core))
    beside = over_y(beside)
    blocks, shard = [own, beside], [2 * z + y, 2 * z + 1 - y]
    q_beside = over_y(q_other)
    for k in range(1, ring // 2 + 1):
        own = over_z(own, 1)
        if k == 1:
            own, beside = lax.optimization_barrier((own, beside))
        if k == 2:
            own, q_beside, w_in, w_down = lax.optimization_barrier((own, q_beside, w_in, w_down))
            beside, q_beside = lax.optimization_barrier((beside, q_beside))
        beside = over_z(beside, 1)
        blocks += [own, beside]
        shard += [2 * (z - k) + y, 2 * (z - k) + 1 - y]
    bases = jnp.stack(shard).astype(jnp.int32) * rows

    local = relative_rows(jnp.arange(rows, dtype=jnp.int32), x, core)
    pos = jnp.concatenate([seq * rows + local, (seq ^ 1) * rows + local])
    bounds = jnp.cumsum(lengths)
    start = jnp.max(jnp.where(bounds[None, :] <= pos[:, None], bounds[None, :], 0), axis=1)
    w_in = lax.optimization_barrier(w_in.transpose(0, 2, 1, 3))
    blocks, w_in, w_down = lax.optimization_barrier((blocks, w_in, w_down))
    weights = (w_in, over_core(w_in)), (w_down, over_core(w_down))
    out = attend(q_own, q_beside, pos[:, None], start[:, None], bases, blocks)
    return out[:rows], over_y(out[rows:]), weights


def expert_kernel(layout, ways, count, first, *refs):
    pieces, refs = refs[: -(len(ways) * 2 + 9)], refs[-(len(ways) * 2 + 9) :]
    ins, downs = refs[:2], refs[2:4]
    outs, (tokens, total, w_in, w_down, sems) = refs[4:-5], refs[-5:]
    owned, width = ins[0].shape[0], ins[0].shape[2]
    copies = []
    for k in range(2 * owned):
        core, e = divmod(k, owned)
        copies.append(
            [
                pltpu.make_async_copy(ins[core].at[e], w_in.at[k % 2], sems.at[0, k]),
                pltpu.make_async_copy(downs[core].at[e], w_down.at[k % 2], sems.at[1, k]),
            ]
        )
        if k < 2:
            for copy in copies[-1]:
                copy.start()
    rows = pieces[0].shape[-2]
    column = lax.broadcasted_iota(jnp.int32, (1, count), 1)
    factors = [[] for _ in range(owned)]
    for i, quarter in enumerate(layout):
        at, start = pl.ds(i * rows, rows), 0
        for index, place in quarter:
            part = pieces[index].at[place] if place else pieces[index]
            size = min(part.shape[1], width - start)
            tokens[at, start : start + size] = part[:, :size]
            start += size
        packed = part[:, size:].astype(F32)
        weight = packed[:, :count] + packed[:, count : 2 * count]
        for e in range(owned):
            chosen = jnp.where(column == first[0] + e, weight, 0.0)
            factors[e].append(jnp.sum(chosen, axis=1, keepdims=True))
    factors = [jnp.concatenate(f, 0) for f in factors]
    for k in range(2 * owned):
        factor = factors[k % owned]
        copies[k][0].wait()
        gate = jnp.dot(tokens[...], w_in[k % 2, 0], preferred_element_type=F32)
        up = jnp.dot(tokens[...], w_in[k % 2, 1], preferred_element_type=F32)
        hidden = gate / (1.0 + jnp.exp(-gate)) * up * factor
        hidden = jnp.where(factor > 0, hidden, 0.0).astype(BF16)
        copies[k][1].wait()
        if k + 2 < 2 * owned:
            copies[k + 2][0].start()
        out = jnp.dot(hidden, w_down[k % 2], preferred_element_type=F32)
        if k == 0:
            total[...] = out
        else:
            total[...] += out
        if k + 2 < 2 * owned:
            copies[k + 2][1].start()
    for k, (group, by, start, size) in enumerate(ways):
        keep, send = outs[2 * k], outs[2 * k + 1]
        for i in range(4):
            at = pl.ds((4 * group + i) * rows, rows)
            y, x = divmod(i, 2)
            part = total[at, start : start + size].astype(BF16)
            if by == "x":
                (send if x else keep)[y] = part
            else:
                (send if y else keep)[x] = part


def experts(first, count, pieces, layout, ways, weights):
    (in_own, in_other), (down_own, down_other) = weights
    owned, _, width, inner = in_own.shape
    rows = pieces[0].shape[-2]
    n = len(layout) * rows
    vmem = pl.BlockSpec(memory_space=pltpu.VMEM)
    return pl.pallas_call(
        functools.partial(expert_kernel, layout, ways, count),
        out_shape=[
            jax.ShapeDtypeStruct((2, rows, size), BF16) for *_, size in ways for _ in range(2)
        ],
        in_specs=[pl.BlockSpec(memory_space=pltpu.SMEM)]
        + [vmem] * len(pieces)
        + [pl.BlockSpec(memory_space=pltpu.HBM)] * 4,
        out_specs=[vmem] * (2 * len(ways)),
        scratch_shapes=[
            pltpu.VMEM((n, width), BF16),
            pltpu.VMEM((n, width), F32),
            pltpu.VMEM((2, 2, width, inner), BF16),
            pltpu.VMEM((2, inner, width), BF16),
            pltpu.SemaphoreType.DMA((2, 2 * owned)),
        ],
        compiler_params=pltpu.CompilerParams(vmem_limit_bytes=VMEM_LIMIT),
        cost_estimate=pl.CostEstimate(
            flops=12 * n * owned * width * inner,
            bytes_accessed=12 * owned * width * inner + 4 * n * width,
            transcendentals=2 * n * owned * inner,
        ),
    )(first, *pieces, in_own, in_other, down_own, down_other)


HALVES = (
    ((0, ()), (1, ())),
    ((4, (0,)), (3, ())),
    ((2, ()), (5, (0,))),
    ((4, (1,)), (5, (1,))),
)
GROUPS = (
    ((0, ()),),
    ((4, (0,)),),
    ((2, ()),),
    ((4, (1,)),),
    ((1, ()),),
    ((3, ()),),
    ((5, (0,)),),
    ((5, (1,)),),
)


def plane_first(a, b):
    return a, b, over_y(a), over_x(b)


def plane_second(a, b, y_a, x_b):
    return a, b, y_a, x_b, over_x(jnp.stack([a, y_a])), over_y(jnp.stack([b, x_b]))


def gather_tokens(unit, use_halves, use_groups):
    half = lax.axis_size("seq") // 4
    middle = (unit.shape[1] - 128) // 2
    own = plane_first(unit[:, :middle], unit[:, middle:])
    up, down, pairs = unit, unit, []
    for _ in range(1, half):
        up, down = over_z(up, 1), over_z(down, -1)
        pairs.append((up, down))
    far_a, far_b = over_z(up[:, :middle], 1), over_z(down[:, middle:], -1)
    own = plane_second(*own)
    pairs = [plane_first(*pair) for pair in pairs]
    far = plane_first(far_a, far_b)
    far, pairs = lax.optimization_barrier((far, pairs))
    far = plane_second(*far)
    pairs = [plane_second(*pair) for pair in pairs]
    own = use_halves(own)
    pairs, own = lax.optimization_barrier((pairs, own))
    pairs = [use_groups(pair) for pair in pairs]
    own = scatter_first(*own)
    own, pairs = lax.optimization_barrier((own, pairs))
    far, pairs = lax.optimization_barrier((far, pairs))
    pairs = [scatter_first(*pair) for pair in pairs]
    far = use_halves(far)
    far, pairs = lax.optimization_barrier((far, pairs))
    far = scatter_first(*far)
    far, pairs = lax.optimization_barrier((far, pairs))
    far = scatter_second(*far)
    pairs = [scatter_second(*pair) for pair in pairs]
    own, far = lax.optimization_barrier((own, far))
    return scatter_second(*own), far, pairs


def scatter_first(a_keep, a_send, b_keep, b_send):
    return add(a_keep, over_x(a_send)), add(b_keep, over_y(b_send))


def scatter_second(a, b):
    return add(a[0], over_y(a[1])), add(b[0], over_x(b[1]))


def mix(own, far, pairs):
    half = lax.axis_size("seq") // 4
    total = jnp.concatenate(own, 1).astype(F32)
    for k, (low, high) in enumerate(pairs):
        total = total + over_z(low, -1 - k).astype(F32) + over_z(high, 1 + k).astype(F32)
    return (total + over_z(jnp.concatenate(far, 1), half).astype(F32)).astype(BF16)


def shards(
    queries, keys, values, lengths, resid, w_out, moe_gain, routes, gates, w_gate_up, w_down
):
    seq, tp = lax.axis_index("seq"), lax.axis_index("tp")
    x, core, y = tp // 2, tp % 2, seq % 2
    rows = resid.shape[0]
    owned = w_gate_up.shape[0]
    count = owned * lax.axis_size("seq")

    own, other, weights = attention(
        queries, keys, values, lengths, seq, x, core, w_gate_up, w_down
    )
    heads = jnp.where(
        y == 0, jnp.concatenate([own, other], 1), jnp.concatenate([other, own], 1)
    )
    received = over_core(
        jnp.dot(heads[2 * rows :], w_out, preferred_element_type=F32).astype(BF16)
    )
    partial = jnp.dot(heads[: 2 * rows], w_out, preferred_element_type=F32)
    partial = partial + received.astype(F32)

    matches = routes[:, :, None] == jnp.arange(count, dtype=jnp.int32)[None, None, :]
    weight = jnp.sum(jnp.where(matches, gates[:, :, None], 0.0), axis=1)
    high = weight.astype(BF16)
    low = (weight - high.astype(F32)).astype(BF16)
    pad = -(-2 * count // 128) * 128 - 2 * count
    packed = jnp.concatenate([high, low, jnp.zeros((rows, pad), BF16)], 1)

    arrived = over_x(partial[rows:].astype(BF16))
    arrived, weights = lax.optimization_barrier((arrived, weights))
    attended = (resid.astype(F32) + partial[:rows] + arrived.astype(F32)).astype(BF16)
    widened = attended.astype(F32)
    meansq = jnp.mean(widened * widened, axis=1, keepdims=True)
    normed = (widened * lax.rsqrt(meansq + 1e-05) * moe_gain[None, :]).astype(BF16)

    first = (owned * seq).astype(jnp.int32).reshape(1)
    half = resid.shape[1] // 2
    halves = ((0, "x", 0, half), (0, "y", half, half))
    groups = ((0, "x", 0, 2 * half), (1, "y", 0, 2 * half))
    return attended, mix(
        *gather_tokens(
            jnp.concatenate([normed, packed], 1),
            lambda pieces: experts(first, count, pieces, HALVES, halves, weights),
            lambda pieces: experts(first, count, pieces, GROUPS, groups, weights),
        )
    )


def solution(mesh):
    return jax.shard_map(
        shards,
        mesh=mesh,
        in_specs=(
            P("seq", "tp"),
            P("seq", "tp"),
            P("seq", "tp"),
            P(),
            P(("seq", "tp"), None),
            P("tp", None),
            P(),
            P(("seq", "tp"), None),
            P(("seq", "tp"), None),
            P("seq", None, None, "tp"),
            P("seq", "tp", None),
        ),
        out_specs=(P(("seq", "tp"), None), P(("seq", "tp"), None)),
        check_vma=False,
    )
```

```python
import functools
import math

import jax
import jax.numpy as jnp
from jax import lax
from jax.experimental import pallas as pl
from jax.experimental.pallas import tpu as pltpu
from jax.sharding import PartitionSpec as P

HEAD_DIM = 128
F32 = jnp.float32
BF16 = jnp.bfloat16
VMEM_LIMIT = 20 * 1024 * 1024


def over_y(a):
    count = lax.axis_size("seq")
    return lax.ppermute(a, "seq", [(i, i ^ 1) for i in range(count)])


def over_z(a, step):
    count = lax.axis_size("seq")
    return lax.ppermute(a, "seq", [(i, (i + 2 * step) % count) for i in range(count)])


def over_x(a):
    return lax.ppermute(a, "tp", [(i, i ^ 2) for i in range(4)])


def over_core(a):
    return lax.ppermute(a, "tp", [(i, i ^ 1) for i in range(4)])


def add(a, b):
    return (a.astype(F32) + b.astype(F32)).astype(BF16)


def relative_rows(a, x, core):
    blocks = a.reshape((2, 2, a.shape[0] // 4) + a.shape[1:])
    blocks = jnp.where(x == 0, blocks, blocks[::-1])
    blocks = jnp.where(core == 0, blocks, blocks[:, ::-1])
    return jnp.swapaxes(blocks, 0, 1).reshape(a.shape)


def attention_kernel(scale, bases, q_own, q_beside, pos_ref, start_ref, *refs):
    kv_refs, out_ref = refs[:-1], refs[-1]
    piece, width = q_own.shape
    key_pos, n = [], 0
    for kv in kv_refs:
        rows = kv.shape[0]
        column = lax.broadcasted_iota(jnp.int32, (1, rows), 1)
        if rows == piece:
            key_pos.append(column + bases[n])
            n += 1
        else:
            key_pos.append(
                jnp.where(column < piece, column + bases[n], column + (bases[n + 1] - piece))
            )
            n += 2
    for part, q_ref in enumerate((q_own, q_beside)):
        rows = pl.ds(part * piece, piece)
        pos, start = pos_ref[rows, :], start_ref[rows, :]
        masks = [(k >= start) & (k <= pos) for k in key_pos]
        for head in range(width // HEAD_DIM):
            lanes = pl.ds(head * HEAD_DIM, HEAD_DIM)
            value_lanes = pl.ds(width + head * HEAD_DIM, HEAD_DIM)
            q = q_ref[:, lanes]
            scores = [
                jnp.where(
                    mask,
                    lax.dot_general(
                        q, kv[:, lanes], (((1,), (1,)), ((), ())), preferred_element_type=F32
                    )
                    * scale,
                    -1e30,
                )
                for kv, mask in zip(kv_refs, masks)
            ]
            top = functools.reduce(jnp.maximum, [jnp.max(v, axis=1, keepdims=True) for v in scores])
            total, mixed = 0.0, 0.0
            for kv, mask, score in zip(kv_refs, masks, scores):
                weight = jnp.where(mask, jnp.exp(score - top), 0.0)
                total = total + jnp.sum(weight, axis=1, keepdims=True)
                mixed = mixed + jnp.dot(
                    weight.astype(BF16), kv[:, value_lanes], preferred_element_type=F32
                )
            out_ref[rows, lanes] = (mixed / total).astype(BF16)


def attend(q, beside, pos, start, bases, blocks):
    vmem = pl.BlockSpec(memory_space=pltpu.VMEM)
    keys = sum(b.shape[0] for b in blocks)
    return pl.pallas_call(
        functools.partial(attention_kernel, 1.0 / math.sqrt(HEAD_DIM)),
        out_shape=jax.ShapeDtypeStruct((2 * q.shape[0], q.shape[1]), BF16),
        in_specs=[pl.BlockSpec(memory_space=pltpu.SMEM)] + [vmem] * (4 + len(blocks)),
        out_specs=vmem,
        compiler_params=pltpu.CompilerParams(vmem_limit_bytes=VMEM_LIMIT),
        cost_estimate=pl.CostEstimate(
            flops=8 * q.size * keys,
            bytes_accessed=8 * q.size + 4 * keys * q.shape[1],
            transcendentals=2 * q.size // HEAD_DIM * keys,
        ),
    )(bases, q, beside, pos, start, *blocks)


def attention(queries, keys, values, lengths, seq, x, core):
    ring = lax.axis_size("seq") // 2
    y, z = seq % 2, seq // 2
    rows, width = queries.shape
    half = width // 2

    def split(a):
        left, right = a[:, :half], a[:, half:]
        return jnp.where(y == 0, left, right), jnp.where(y == 0, right, left)

    (k_own, k_other), (v_own, v_other) = split(keys), split(values)
    own, beside = jnp.concatenate([k_own, v_own], 1), jnp.concatenate([k_other, v_other], 1)
    own, beside, queries = lax.optimization_barrier((own, beside, queries))
    q_own, q_other = split(relative_rows(queries, x, core))
    beside = over_y(beside)
    blocks, shard = [own, beside], [2 * z + y, 2 * z + 1 - y]
    q_beside = over_y(q_other)
    for k in range(1, ring // 2 + 1):
        own = over_z(own, 1)
        if k == 1:
            own, beside = lax.optimization_barrier((own, beside))
        if k == 2:
            beside, q_beside = lax.optimization_barrier((beside, q_beside))
        beside = over_z(beside, 1)
        blocks += [own, beside]
        shard += [2 * (z - k) + y, 2 * (z - k) + 1 - y]
    bases = jnp.stack(shard).astype(jnp.int32) * rows

    local = relative_rows(jnp.arange(rows, dtype=jnp.int32), x, core)
    pos = jnp.concatenate([seq * rows + local, (seq ^ 1) * rows + local])
    bounds = jnp.cumsum(lengths)
    start = jnp.max(jnp.where(bounds[None, :] <= pos[:, None], bounds[None, :], 0), axis=1)
    out = attend(q_own, q_beside, pos[:, None], start[:, None], bases, blocks)
    return out[:rows], over_y(out[rows:])


def expert_kernel(layout, ways, count, first, *refs):
    pieces, refs = refs[: -(len(ways) * 2 + 9)], refs[-(len(ways) * 2 + 9) :]
    ins, downs = refs[:2], refs[2:4]
    outs, (tokens, total, w_in, w_down, sems) = refs[4:-5], refs[-5:]
    owned, width = ins[0].shape[0], ins[0].shape[2]
    copies = []
    for k in range(2 * owned):
        core, e = divmod(k, owned)
        copies.append(
            [
                pltpu.make_async_copy(ins[core].at[e], w_in.at[k % 2], sems.at[0, k]),
                pltpu.make_async_copy(downs[core].at[e], w_down.at[k % 2], sems.at[1, k]),
            ]
        )
        if k < 2:
            for copy in copies[-1]:
                copy.start()
    rows = pieces[0].shape[-2]
    column = lax.broadcasted_iota(jnp.int32, (1, count), 1)
    factors = [[] for _ in range(owned)]
    for i, quarter in enumerate(layout):
        at, start = pl.ds(i * rows, rows), 0
        for index, place in quarter:
            part = pieces[index].at[place] if place else pieces[index]
            size = min(part.shape[1], width - start)
            tokens[at, start : start + size] = part[:, :size]
            start += size
        packed = part[:, size:].astype(F32)
        weight = packed[:, :count] + packed[:, count : 2 * count]
        for e in range(owned):
            chosen = jnp.where(column == first[0] + e, weight, 0.0)
            factors[e].append(jnp.sum(chosen, axis=1, keepdims=True))
    factors = [jnp.concatenate(f, 0) for f in factors]
    for k in range(2 * owned):
        factor = factors[k % owned]
        copies[k][0].wait()
        gate = jnp.dot(tokens[...], w_in[k % 2, 0], preferred_element_type=F32)
        up = jnp.dot(tokens[...], w_in[k % 2, 1], preferred_element_type=F32)
        hidden = gate / (1.0 + jnp.exp(-gate)) * up * factor
        hidden = jnp.where(factor > 0, hidden, 0.0).astype(BF16)
        copies[k][1].wait()
        if k + 2 < 2 * owned:
            copies[k + 2][0].start()
        out = jnp.dot(hidden, w_down[k % 2], preferred_element_type=F32)
        if k == 0:
            total[...] = out
        else:
            total[...] += out
        if k + 2 < 2 * owned:
            copies[k + 2][1].start()
    for k, (group, by, start, size) in enumerate(ways):
        keep, send = outs[2 * k], outs[2 * k + 1]
        for i in range(4):
            at = pl.ds((4 * group + i) * rows, rows)
            y, x = divmod(i, 2)
            part = total[at, start : start + size].astype(BF16)
            if by == "x":
                (send if x else keep)[y] = part
            else:
                (send if y else keep)[x] = part


def experts(first, count, pieces, layout, ways, weights):
    (in_own, in_other), (down_own, down_other) = weights
    owned, _, width, inner = in_own.shape
    rows = pieces[0].shape[-2]
    n = len(layout) * rows
    vmem = pl.BlockSpec(memory_space=pltpu.VMEM)
    return pl.pallas_call(
        functools.partial(expert_kernel, layout, ways, count),
        out_shape=[
            jax.ShapeDtypeStruct((2, rows, size), BF16) for *_, size in ways for _ in range(2)
        ],
        in_specs=[pl.BlockSpec(memory_space=pltpu.SMEM)]
        + [vmem] * len(pieces)
        + [pl.BlockSpec(memory_space=pltpu.HBM)] * 4,
        out_specs=[vmem] * (2 * len(ways)),
        scratch_shapes=[
            pltpu.VMEM((n, width), BF16),
            pltpu.VMEM((n, width), F32),
            pltpu.VMEM((2, 2, width, inner), BF16),
            pltpu.VMEM((2, inner, width), BF16),
            pltpu.SemaphoreType.DMA((2, 2 * owned)),
        ],
        compiler_params=pltpu.CompilerParams(vmem_limit_bytes=VMEM_LIMIT),
        cost_estimate=pl.CostEstimate(
            flops=12 * n * owned * width * inner,
            bytes_accessed=12 * owned * width * inner + 4 * n * width,
            transcendentals=2 * n * owned * inner,
        ),
    )(first, *pieces, in_own, in_other, down_own, down_other)


HALVES = (
    ((0, ()), (1, ())),
    ((4, (0,)), (3, ())),
    ((2, ()), (5, (0,))),
    ((4, (1,)), (5, (1,))),
)
GROUPS = (
    ((0, ()),),
    ((4, (0,)),),
    ((2, ()),),
    ((4, (1,)),),
    ((1, ()),),
    ((3, ()),),
    ((5, (0,)),),
    ((5, (1,)),),
)


def plane_first(a, b):
    return a, b, over_y(a), over_x(b)


def plane_second(a, b, y_a, x_b):
    return a, b, y_a, x_b, over_x(jnp.stack([a, y_a])), over_y(jnp.stack([b, x_b]))


def gather_tokens(unit, use_halves, use_groups):
    half = lax.axis_size("seq") // 4
    middle = (unit.shape[1] - 128) // 2
    own = plane_first(unit[:, :middle], unit[:, middle:])
    up, down, pairs = unit, unit, []
    for _ in range(1, half):
        up, down = over_z(up, 1), over_z(down, -1)
        pairs.append((up, down))
    far_a, far_b = over_z(up[:, :middle], 1), over_z(down[:, middle:], -1)
    own = plane_second(*own)
    pairs = [plane_first(*pair) for pair in pairs]
    far_a, far_b, pairs = lax.optimization_barrier((far_a, far_b, pairs))
    far = plane_first(far_a, far_b)
    pairs = [plane_second(*pair) for pair in pairs]
    far, own = lax.optimization_barrier((far, own))
    far = plane_second(*far)
    own = use_halves(own)
    pairs, own = lax.optimization_barrier((pairs, own))
    pairs = [use_groups(pair) for pair in pairs]
    own = scatter_first(*own)
    own, pairs = lax.optimization_barrier((own, pairs))
    far, pairs = lax.optimization_barrier((far, pairs))
    pairs = [scatter_first(*pair) for pair in pairs]
    far = use_halves(far)
    far, pairs = lax.optimization_barrier((far, pairs))
    far = scatter_first(*far)
    far, pairs = lax.optimization_barrier((far, pairs))
    far = scatter_second(*far)
    pairs = [scatter_second(*pair) for pair in pairs]
    own, far = lax.optimization_barrier((own, far))
    return scatter_second(*own), far, pairs


def scatter_first(a_keep, a_send, b_keep, b_send):
    return add(a_keep, over_x(a_send)), add(b_keep, over_y(b_send))


def scatter_second(a, b):
    return add(a[0], over_y(a[1])), add(b[0], over_x(b[1]))


def mix(own, far, pairs):
    half = lax.axis_size("seq") // 4
    total = jnp.concatenate(own, 1).astype(F32)
    for k, (low, high) in enumerate(pairs):
        total = total + over_z(low, -1 - k).astype(F32) + over_z(high, 1 + k).astype(F32)
    return (total + over_z(jnp.concatenate(far, 1), half).astype(F32)).astype(BF16)


def shards(
    queries, keys, values, lengths, resid, w_out, moe_gain, routes, gates, w_gate_up, w_down
):
    seq, tp = lax.axis_index("seq"), lax.axis_index("tp")
    x, core, y = tp // 2, tp % 2, seq % 2
    rows = resid.shape[0]
    owned = w_gate_up.shape[0]
    count = owned * lax.axis_size("seq")

    own, other = attention(queries, keys, values, lengths, seq, x, core)
    heads = jnp.where(
        y == 0, jnp.concatenate([own, other], 1), jnp.concatenate([other, own], 1)
    )
    received = over_core(
        jnp.dot(heads[2 * rows :], w_out, preferred_element_type=F32).astype(BF16)
    )
    partial = jnp.dot(heads[: 2 * rows], w_out, preferred_element_type=F32)
    received, w_in = lax.optimization_barrier((received, w_gate_up))
    w_in = lax.optimization_barrier(w_in.transpose(0, 2, 1, 3))
    partial = partial + received.astype(F32)

    matches = routes[:, :, None] == jnp.arange(count, dtype=jnp.int32)[None, None, :]
    weight = jnp.sum(jnp.where(matches, gates[:, :, None], 0.0), axis=1)
    high = weight.astype(BF16)
    low = (weight - high.astype(F32)).astype(BF16)
    pad = -(-2 * count // 128) * 128 - 2 * count
    packed = jnp.concatenate([high, low, jnp.zeros((rows, pad), BF16)], 1)

    arrived = over_x(partial[rows:].astype(BF16))
    arrived, w_in, w_down = lax.optimization_barrier((arrived, w_in, w_down))
    weights = (w_in, over_core(w_in)), (w_down, over_core(w_down))
    attended = (resid.astype(F32) + partial[:rows] + arrived.astype(F32)).astype(BF16)
    widened = attended.astype(F32)
    meansq = jnp.mean(widened * widened, axis=1, keepdims=True)
    normed = (widened * lax.rsqrt(meansq + 1e-05) * moe_gain[None, :]).astype(BF16)

    first = (owned * seq).astype(jnp.int32).reshape(1)
    half = resid.shape[1] // 2
    halves = ((0, "x", 0, half), (0, "y", half, half))
    groups = ((0, "x", 0, 2 * half), (1, "y", 0, 2 * half))
    return attended, mix(
        *gather_tokens(
            jnp.concatenate([normed, packed], 1),
            lambda pieces: experts(first, count, pieces, HALVES, halves, weights),
            lambda pieces: experts(first, count, pieces, GROUPS, groups, weights),
        )
    )


def solution(mesh):
    return jax.shard_map(
        shards,
        mesh=mesh,
        in_specs=(
            P("seq", "tp"),
            P("seq", "tp"),
            P("seq", "tp"),
            P(),
            P(("seq", "tp"), None),
            P("tp", None),
            P(),
            P(("seq", "tp"), None),
            P(("seq", "tp"), None),
            P("seq", None, None, "tp"),
            P("seq", "tp", None),
        ),
        out_specs=(P(("seq", "tp"), None), P(("seq", "tp"), None)),
        check_vma=False,
    )
```

```python
import functools
import math

import jax
import jax.numpy as jnp
from jax import lax
from jax.experimental import pallas as pl
from jax.experimental.pallas import tpu as pltpu
from jax.sharding import PartitionSpec as P

HEAD_DIM = 128
F32 = jnp.float32
BF16 = jnp.bfloat16
VMEM_LIMIT = 20 * 1024 * 1024


def over_y(a):
    count = lax.axis_size("seq")
    return lax.ppermute(a, "seq", [(i, i ^ 1) for i in range(count)])


def over_z(a, step):
    count = lax.axis_size("seq")
    return lax.ppermute(a, "seq", [(i, (i + 2 * step) % count) for i in range(count)])


def across_z(a, k):
    count = lax.axis_size("seq")
    return lax.ppermute(a, "seq", [(i, i ^ (2 * k)) for i in range(count)])


def over_x(a):
    return lax.ppermute(a, "tp", [(i, i ^ 2) for i in range(4)])


def over_core(a):
    return lax.ppermute(a, "tp", [(i, i ^ 1) for i in range(4)])


def add(a, b):
    return (a.astype(F32) + b.astype(F32)).astype(BF16)


def relative_rows(a, x, core):
    blocks = a.reshape((2, 2, a.shape[0] // 4) + a.shape[1:])
    blocks = jnp.where(x == 0, blocks, blocks[::-1])
    blocks = jnp.where(core == 0, blocks, blocks[:, ::-1])
    return jnp.swapaxes(blocks, 0, 1).reshape(a.shape)


def attention_kernel(scale, bases, q_own, q_beside, pos_ref, start_ref, *refs):
    kv_refs, out_ref = refs[:-1], refs[-1]
    piece, width = q_own.shape
    key_pos, n = [], 0
    for kv in kv_refs:
        rows = kv.shape[0]
        column = lax.broadcasted_iota(jnp.int32, (1, rows), 1)
        if rows == piece:
            key_pos.append(column + bases[n])
            n += 1
        else:
            key_pos.append(
                jnp.where(column < piece, column + bases[n], column + (bases[n + 1] - piece))
            )
            n += 2
    for part, q_ref in enumerate((q_own, q_beside)):
        rows = pl.ds(part * piece, piece)
        pos, start = pos_ref[rows, :], start_ref[rows, :]
        masks = [(k >= start) & (k <= pos) for k in key_pos]
        for head in range(width // HEAD_DIM):
            lanes = pl.ds(head * HEAD_DIM, HEAD_DIM)
            value_lanes = pl.ds(width + head * HEAD_DIM, HEAD_DIM)
            q = q_ref[:, lanes]
            scores = [
                jnp.where(
                    mask,
                    lax.dot_general(
                        q, kv[:, lanes], (((1,), (1,)), ((), ())), preferred_element_type=F32
                    )
                    * scale,
                    -1e30,
                )
                for kv, mask in zip(kv_refs, masks)
            ]
            top = functools.reduce(jnp.maximum, [jnp.max(v, axis=1, keepdims=True) for v in scores])
            total, mixed = 0.0, 0.0
            for kv, mask, score in zip(kv_refs, masks, scores):
                weight = jnp.where(mask, jnp.exp(score - top), 0.0)
                total = total + jnp.sum(weight, axis=1, keepdims=True)
                mixed = mixed + jnp.dot(
                    weight.astype(BF16), kv[:, value_lanes], preferred_element_type=F32
                )
            out_ref[rows, lanes] = (mixed / total).astype(BF16)


def attend(q, beside, pos, start, bases, blocks):
    vmem = pl.BlockSpec(memory_space=pltpu.VMEM)
    keys = sum(b.shape[0] for b in blocks)
    return pl.pallas_call(
        functools.partial(attention_kernel, 1.0 / math.sqrt(HEAD_DIM)),
        out_shape=jax.ShapeDtypeStruct((2 * q.shape[0], q.shape[1]), BF16),
        in_specs=[pl.BlockSpec(memory_space=pltpu.SMEM)] + [vmem] * (4 + len(blocks)),
        out_specs=vmem,
        compiler_params=pltpu.CompilerParams(vmem_limit_bytes=VMEM_LIMIT),
        cost_estimate=pl.CostEstimate(
            flops=8 * q.size * keys,
            bytes_accessed=8 * q.size + 4 * keys * q.shape[1],
            transcendentals=2 * q.size // HEAD_DIM * keys,
        ),
    )(bases, q, beside, pos, start, *blocks)


def attention(queries, keys, values, lengths, seq, x, core, held):
    ring = lax.axis_size("seq") // 2
    y, z = seq % 2, seq // 2
    rows, width = queries.shape
    half = width // 2

    def split(a):
        left, right = a[:, :half], a[:, half:]
        return jnp.where(y == 0, left, right), jnp.where(y == 0, right, left)

    (k_own, k_other), (v_own, v_other) = split(keys), split(values)
    own, beside = jnp.concatenate([k_own, v_own], 1), jnp.concatenate([k_other, v_other], 1)
    own, beside, queries = lax.optimization_barrier((own, beside, queries))
    q_own, q_other = split(relative_rows(queries, x, core))
    beside = over_y(beside)
    blocks, shard = [own, beside], [2 * z + y, 2 * z + 1 - y]
    q_beside = over_y(q_other)
    for k in range(1, ring // 2 + 1):
        own = over_z(own, 1)
        if k == 1:
            own, beside = lax.optimization_barrier((own, beside))
        if k == 2:
            beside, q_beside = lax.optimization_barrier((beside, q_beside))
        beside = over_z(beside, 1)
        blocks += [own, beside]
        shard += [2 * (z - k) + y, 2 * (z - k) + 1 - y]
    bases = jnp.stack(shard).astype(jnp.int32) * rows

    local = relative_rows(jnp.arange(rows, dtype=jnp.int32), x, core)
    pos = jnp.concatenate([seq * rows + local, (seq ^ 1) * rows + local])
    bounds = jnp.cumsum(lengths)
    start = jnp.max(jnp.where(bounds[None, :] <= pos[:, None], bounds[None, :], 0), axis=1)
    blocks, held = lax.optimization_barrier((blocks, held))
    out = attend(q_own, q_beside, pos[:, None], start[:, None], bases, blocks)
    return out[:rows], over_y(out[rows:]), held


def expert_kernel(layout, ways, count, first, *refs):
    pieces, refs = refs[: -(len(ways) * 2 + 9)], refs[-(len(ways) * 2 + 9) :]
    ins, downs = refs[:2], refs[2:4]
    outs, (tokens, total, w_in, w_down, sems) = refs[4:-5], refs[-5:]
    owned, width = ins[0].shape[0], ins[0].shape[2]
    copies = []
    for k in range(2 * owned):
        core, e = divmod(k, owned)
        copies.append(
            [
                pltpu.make_async_copy(ins[core].at[e], w_in.at[k % 2], sems.at[0, k]),
                pltpu.make_async_copy(downs[core].at[e], w_down.at[k % 2], sems.at[1, k]),
            ]
        )
        if k < 2:
            for copy in copies[-1]:
                copy.start()
    rows = pieces[0].shape[-2]
    column = lax.broadcasted_iota(jnp.int32, (1, count), 1)
    factors = [[] for _ in range(owned)]
    for i, quarter in enumerate(layout):
        at, start = pl.ds(i * rows, rows), 0
        for index, place in quarter:
            part = pieces[index].at[place] if place else pieces[index]
            size = min(part.shape[1], width - start)
            tokens[at, start : start + size] = part[:, :size]
            start += size
        packed = part[:, size:].astype(F32)
        weight = packed[:, :count] + packed[:, count : 2 * count]
        for e in range(owned):
            chosen = jnp.where(column == first[0] + e, weight, 0.0)
            factors[e].append(jnp.sum(chosen, axis=1, keepdims=True))
    factors = [jnp.concatenate(f, 0) for f in factors]
    for k in range(2 * owned):
        factor = factors[k % owned]
        copies[k][0].wait()
        gate = jnp.dot(tokens[...], w_in[k % 2, 0], preferred_element_type=F32)
        up = jnp.dot(tokens[...], w_in[k % 2, 1], preferred_element_type=F32)
        hidden = gate / (1.0 + jnp.exp(-gate)) * up * factor
        hidden = jnp.where(factor > 0, hidden, 0.0).astype(BF16)
        copies[k][1].wait()
        if k + 2 < 2 * owned:
            copies[k + 2][0].start()
        out = jnp.dot(hidden, w_down[k % 2], preferred_element_type=F32)
        if k == 0:
            total[...] = out
        else:
            total[...] += out
        if k + 2 < 2 * owned:
            copies[k + 2][1].start()
    for k, (group, by, start, size) in enumerate(ways):
        keep, send = outs[2 * k], outs[2 * k + 1]
        for i in range(4):
            at = pl.ds((4 * group + i) * rows, rows)
            y, x = divmod(i, 2)
            part = total[at, start : start + size].astype(BF16)
            if by == "x":
                (send if x else keep)[y] = part
            else:
                (send if y else keep)[x] = part


def experts(first, count, pieces, layout, ways, weights):
    (in_own, in_other), (down_own, down_other) = weights
    owned, _, width, inner = in_own.shape
    rows = pieces[0].shape[-2]
    n = len(layout) * rows
    vmem = pl.BlockSpec(memory_space=pltpu.VMEM)
    return pl.pallas_call(
        functools.partial(expert_kernel, layout, ways, count),
        out_shape=[
            jax.ShapeDtypeStruct((2, rows, size), BF16) for *_, size in ways for _ in range(2)
        ],
        in_specs=[pl.BlockSpec(memory_space=pltpu.SMEM)]
        + [vmem] * len(pieces)
        + [pl.BlockSpec(memory_space=pltpu.HBM)] * 4,
        out_specs=[vmem] * (2 * len(ways)),
        scratch_shapes=[
            pltpu.VMEM((n, width), BF16),
            pltpu.VMEM((n, width), F32),
            pltpu.VMEM((2, 2, width, inner), BF16),
            pltpu.VMEM((2, inner, width), BF16),
            pltpu.SemaphoreType.DMA((2, 2 * owned)),
        ],
        compiler_params=pltpu.CompilerParams(vmem_limit_bytes=VMEM_LIMIT),
        cost_estimate=pl.CostEstimate(
            flops=12 * n * owned * width * inner,
            bytes_accessed=12 * owned * width * inner + 4 * n * width,
            transcendentals=2 * n * owned * inner,
        ),
    )(first, *pieces, in_own, in_other, down_own, down_other)


HALVES = (
    ((0, ()), (1, ())),
    ((4, (0,)), (3, ())),
    ((2, ()), (5, (0,))),
    ((4, (1,)), (5, (1,))),
)
GROUPS = (
    ((0, ()),),
    ((4, (0,)),),
    ((2, ()),),
    ((4, (1,)),),
    ((1, ()),),
    ((3, ()),),
    ((5, (0,)),),
    ((5, (1,)),),
)


def plane_first(a, b):
    return a, b, over_y(a), over_x(b)


def plane_second(a, b, y_a, x_b):
    return a, b, y_a, x_b, over_x(jnp.stack([a, y_a])), over_y(jnp.stack([b, x_b]))


def partners():
    return [(3, 1)] + [(k, k + 1) for k in range(4, lax.axis_size("seq") // 2, 2)]


def gather_tokens(unit, use_halves, use_groups):
    middle = (unit.shape[1] - 128) // 2
    own = plane_first(unit[:, :middle], unit[:, middle:])
    pairs = [[across_z(unit, k) for k in pair] for pair in partners()]
    relayed = pairs[0][0]
    far_a, far_b = across_z(relayed[:, :middle], 1), across_z(relayed[:, middle:], 1)
    own = plane_second(*own)
    pairs = [plane_first(*pair) for pair in pairs]
    far_a, far_b, pairs = lax.optimization_barrier((far_a, far_b, pairs))
    far = plane_first(far_a, far_b)
    pairs = [plane_second(*pair) for pair in pairs]
    far, own = lax.optimization_barrier((far, own))
    far = plane_second(*far)
    own = use_halves(own)
    pairs, own = lax.optimization_barrier((pairs, own))
    pairs = [use_groups(pair) for pair in pairs]
    own = scatter_first(*own)
    own, pairs = lax.optimization_barrier((own, pairs))
    far, pairs = lax.optimization_barrier((far, pairs))
    pairs = [scatter_first(*pair) for pair in pairs]
    far = use_halves(far)
    far, pairs = lax.optimization_barrier((far, pairs))
    pairs = [scatter_second(*pair) for pair in pairs]
    far = scatter_first(*far)
    own = scatter_second(*own)
    far, own, pairs = lax.optimization_barrier((far, own, pairs))
    far = scatter_second(*far)
    return own, far, pairs


def scatter_first(a_keep, a_send, b_keep, b_send):
    return add(a_keep, over_x(a_send)), add(b_keep, over_y(b_send))


def scatter_second(a, b):
    return add(a[0], over_y(a[1])), add(b[0], over_x(b[1]))


def mix(own, far, pairs):
    total = jnp.concatenate(own, 1).astype(F32)
    for pair, ways in zip(pairs, partners()):
        for part, k in zip(pair, ways):
            total = total + across_z(part, k).astype(F32)
    return (total + across_z(jnp.concatenate(far, 1), 2).astype(F32)).astype(BF16)


def shards(
    queries, keys, values, lengths, resid, w_out, moe_gain, routes, gates, w_gate_up, w_down
):
    seq, tp = lax.axis_index("seq"), lax.axis_index("tp")
    x, core, y = tp // 2, tp % 2, seq % 2
    rows = resid.shape[0]
    owned = w_gate_up.shape[0]
    count = owned * lax.axis_size("seq")

    own, other, down_other = attention(
        queries, keys, values, lengths, seq, x, core, over_core(w_down)
    )
    heads = jnp.where(
        y == 0, jnp.concatenate([own, other], 1), jnp.concatenate([other, own], 1)
    )
    received = over_core(
        jnp.dot(heads[2 * rows :], w_out, preferred_element_type=F32).astype(BF16)
    )
    partial = jnp.dot(heads[: 2 * rows], w_out, preferred_element_type=F32)
    received, w_in = lax.optimization_barrier((received, w_gate_up))
    w_in = lax.optimization_barrier(w_in.transpose(0, 2, 1, 3))
    partial = partial + received.astype(F32)

    matches = routes[:, :, None] == jnp.arange(count, dtype=jnp.int32)[None, None, :]
    weight = jnp.sum(jnp.where(matches, gates[:, :, None], 0.0), axis=1)
    high = weight.astype(BF16)
    low = (weight - high.astype(F32)).astype(BF16)
    pad = -(-2 * count // 128) * 128 - 2 * count
    packed = jnp.concatenate([high, low, jnp.zeros((rows, pad), BF16)], 1)

    arrived = over_x(partial[rows:].astype(BF16))
    arrived, w_in = lax.optimization_barrier((arrived, w_in))
    weights = (w_in, over_core(w_in)), (w_down, down_other)
    attended = (resid.astype(F32) + partial[:rows] + arrived.astype(F32)).astype(BF16)
    widened = attended.astype(F32)
    meansq = jnp.mean(widened * widened, axis=1, keepdims=True)
    normed = (widened * lax.rsqrt(meansq + 1e-05) * moe_gain[None, :]).astype(BF16)

    first = (owned * seq).astype(jnp.int32).reshape(1)
    half = resid.shape[1] // 2
    halves = ((0, "x", 0, half), (0, "y", half, half))
    groups = ((0, "x", 0, 2 * half), (1, "y", 0, 2 * half))
    return attended, mix(
        *gather_tokens(
            jnp.concatenate([normed, packed], 1),
            lambda pieces: experts(first, count, pieces, HALVES, halves, weights),
            lambda pieces: experts(first, count, pieces, GROUPS, groups, weights),
        )
    )


def solution(mesh):
    return jax.shard_map(
        shards,
        mesh=mesh,
        in_specs=(
            P("seq", "tp"),
            P("seq", "tp"),
            P("seq", "tp"),
            P(),
            P(("seq", "tp"), None),
            P("tp", None),
            P(),
            P(("seq", "tp"), None),
            P(("seq", "tp"), None),
            P("seq", None, None, "tp"),
            P("seq", "tp", None),
        ),
        out_specs=(P(("seq", "tp"), None), P(("seq", "tp"), None)),
        check_vma=False,
    )
```

```python
import functools
import math

import jax
import jax.numpy as jnp
from jax import lax
from jax.experimental import pallas as pl
from jax.experimental.pallas import tpu as pltpu
from jax.sharding import PartitionSpec as P

HEAD_DIM = 128
F32 = jnp.float32
BF16 = jnp.bfloat16
VMEM_LIMIT = 20 * 1024 * 1024


def over_y(a):
    count = lax.axis_size("seq")
    return lax.ppermute(a, "seq", [(i, i ^ 1) for i in range(count)])


def over_z(a, step):
    count = lax.axis_size("seq")
    return lax.ppermute(a, "seq", [(i, (i + 2 * step) % count) for i in range(count)])


def across_z(a, k):
    count = lax.axis_size("seq")
    return lax.ppermute(a, "seq", [(i, i ^ (2 * k)) for i in range(count)])


def over_x(a):
    return lax.ppermute(a, "tp", [(i, i ^ 2) for i in range(4)])


def over_core(a):
    return lax.ppermute(a, "tp", [(i, i ^ 1) for i in range(4)])


def add(a, b):
    return (a.astype(F32) + b.astype(F32)).astype(BF16)


def relative_rows(a, x, core):
    blocks = a.reshape((2, 2, a.shape[0] // 4) + a.shape[1:])
    blocks = jnp.where(x == 0, blocks, blocks[::-1])
    blocks = jnp.where(core == 0, blocks, blocks[:, ::-1])
    return jnp.swapaxes(blocks, 0, 1).reshape(a.shape)


def attention_kernel(scale, bases, q_own, q_beside, pos_ref, start_ref, *refs):
    kv_refs, out_ref = refs[:-1], refs[-1]
    piece, width = q_own.shape
    key_pos, n = [], 0
    for kv in kv_refs:
        rows = kv.shape[0]
        column = lax.broadcasted_iota(jnp.int32, (1, rows), 1)
        if rows == piece:
            key_pos.append(column + bases[n])
            n += 1
        else:
            key_pos.append(
                jnp.where(column < piece, column + bases[n], column + (bases[n + 1] - piece))
            )
            n += 2
    for part, q_ref in enumerate((q_own, q_beside)):
        rows = pl.ds(part * piece, piece)
        pos, start = pos_ref[rows, :], start_ref[rows, :]
        masks = [(k >= start) & (k <= pos) for k in key_pos]
        for head in range(width // HEAD_DIM):
            lanes = pl.ds(head * HEAD_DIM, HEAD_DIM)
            value_lanes = pl.ds(width + head * HEAD_DIM, HEAD_DIM)
            q = q_ref[:, lanes]
            scores = [
                jnp.where(
                    mask,
                    lax.dot_general(
                        q, kv[:, lanes], (((1,), (1,)), ((), ())), preferred_element_type=F32
                    )
                    * scale,
                    -1e30,
                )
                for kv, mask in zip(kv_refs, masks)
            ]
            top = functools.reduce(jnp.maximum, [jnp.max(v, axis=1, keepdims=True) for v in scores])
            total, mixed = 0.0, 0.0
            for kv, mask, score in zip(kv_refs, masks, scores):
                weight = jnp.where(mask, jnp.exp(score - top), 0.0)
                total = total + jnp.sum(weight, axis=1, keepdims=True)
                mixed = mixed + jnp.dot(
                    weight.astype(BF16), kv[:, value_lanes], preferred_element_type=F32
                )
            out_ref[rows, lanes] = (mixed / total).astype(BF16)


def attend(q, beside, pos, start, bases, blocks):
    vmem = pl.BlockSpec(memory_space=pltpu.VMEM)
    keys = sum(b.shape[0] for b in blocks)
    return pl.pallas_call(
        functools.partial(attention_kernel, 1.0 / math.sqrt(HEAD_DIM)),
        out_shape=jax.ShapeDtypeStruct((2 * q.shape[0], q.shape[1]), BF16),
        in_specs=[pl.BlockSpec(memory_space=pltpu.SMEM)] + [vmem] * (4 + len(blocks)),
        out_specs=vmem,
        compiler_params=pltpu.CompilerParams(vmem_limit_bytes=VMEM_LIMIT),
        cost_estimate=pl.CostEstimate(
            flops=8 * q.size * keys,
            bytes_accessed=8 * q.size + 4 * keys * q.shape[1],
            transcendentals=2 * q.size // HEAD_DIM * keys,
        ),
    )(bases, q, beside, pos, start, *blocks)


def attention(queries, keys, values, lengths, seq, x, core, held):
    ring = lax.axis_size("seq") // 2
    y, z = seq % 2, seq // 2
    rows, width = queries.shape
    half = width // 2

    def split(a):
        left, right = a[:, :half], a[:, half:]
        return jnp.where(y == 0, left, right), jnp.where(y == 0, right, left)

    (k_own, k_other), (v_own, v_other) = split(keys), split(values)
    own, beside = jnp.concatenate([k_own, v_own], 1), jnp.concatenate([k_other, v_other], 1)
    own, beside, queries, held = lax.optimization_barrier((own, beside, queries, held))
    q_own, q_other = split(relative_rows(queries, x, core))
    beside = over_y(beside)
    blocks, shard = [own, beside], [2 * z + y, 2 * z + 1 - y]
    q_beside = over_y(q_other)
    for k in range(1, ring // 2 + 1):
        own = over_z(own, 1)
        if k == 1:
            own, beside = lax.optimization_barrier((own, beside))
        if k == 2:
            beside, q_beside = lax.optimization_barrier((beside, q_beside))
        beside = over_z(beside, 1)
        blocks += [own, beside]
        shard += [2 * (z - k) + y, 2 * (z - k) + 1 - y]
    bases = jnp.stack(shard).astype(jnp.int32) * rows

    local = relative_rows(jnp.arange(rows, dtype=jnp.int32), x, core)
    pos = jnp.concatenate([seq * rows + local, (seq ^ 1) * rows + local])
    bounds = jnp.cumsum(lengths)
    start = jnp.max(jnp.where(bounds[None, :] <= pos[:, None], bounds[None, :], 0), axis=1)
    blocks, held = lax.optimization_barrier((blocks, over_core(held)))
    out = attend(q_own, q_beside, pos[:, None], start[:, None], bases, blocks)
    return out[:rows], over_y(out[rows:]), held


def expert_kernel(layout, ways, count, first, *refs):
    pieces, refs = refs[: -(len(ways) * 2 + 9)], refs[-(len(ways) * 2 + 9) :]
    ins, downs = refs[:2], refs[2:4]
    outs, (tokens, total, w_in, w_down, sems) = refs[4:-5], refs[-5:]
    owned, width = ins[0].shape[0], ins[0].shape[2]
    copies = []
    for k in range(2 * owned):
        core, e = divmod(k, owned)
        copies.append(
            [
                pltpu.make_async_copy(ins[core].at[e], w_in.at[k % 2], sems.at[0, k]),
                pltpu.make_async_copy(downs[core].at[e], w_down.at[k % 2], sems.at[1, k]),
            ]
        )
        if k < 2:
            for copy in copies[-1]:
                copy.start()
    rows = pieces[0].shape[-2]
    column = lax.broadcasted_iota(jnp.int32, (1, count), 1)
    factors = [[] for _ in range(owned)]
    for i, quarter in enumerate(layout):
        at, start = pl.ds(i * rows, rows), 0
        for index, place in quarter:
            part = pieces[index].at[place] if place else pieces[index]
            size = min(part.shape[1], width - start)
            tokens[at, start : start + size] = part[:, :size]
            start += size
        packed = part[:, size:].astype(F32)
        weight = packed[:, :count] + packed[:, count : 2 * count]
        for e in range(owned):
            chosen = jnp.where(column == first[0] + e, weight, 0.0)
            factors[e].append(jnp.sum(chosen, axis=1, keepdims=True))
    factors = [jnp.concatenate(f, 0) for f in factors]
    for k in range(2 * owned):
        factor = factors[k % owned]
        copies[k][0].wait()
        gate = jnp.dot(tokens[...], w_in[k % 2, 0], preferred_element_type=F32)
        up = jnp.dot(tokens[...], w_in[k % 2, 1], preferred_element_type=F32)
        hidden = gate / (1.0 + jnp.exp(-gate)) * up * factor
        hidden = jnp.where(factor > 0, hidden, 0.0).astype(BF16)
        copies[k][1].wait()
        if k + 2 < 2 * owned:
            copies[k + 2][0].start()
        out = jnp.dot(hidden, w_down[k % 2], preferred_element_type=F32)
        if k == 0:
            total[...] = out
        else:
            total[...] += out
        if k + 2 < 2 * owned:
            copies[k + 2][1].start()
    for k, (group, by, start, size) in enumerate(ways):
        keep, send = outs[2 * k], outs[2 * k + 1]
        for i in range(4):
            at = pl.ds((4 * group + i) * rows, rows)
            y, x = divmod(i, 2)
            part = total[at, start : start + size].astype(BF16)
            if by == "x":
                (send if x else keep)[y] = part
            else:
                (send if y else keep)[x] = part


def experts(first, count, pieces, layout, ways, weights):
    (in_own, in_other), (down_own, down_other) = weights
    owned, _, width, inner = in_own.shape
    rows = pieces[0].shape[-2]
    n = len(layout) * rows
    vmem = pl.BlockSpec(memory_space=pltpu.VMEM)
    return pl.pallas_call(
        functools.partial(expert_kernel, layout, ways, count),
        out_shape=[
            jax.ShapeDtypeStruct((2, rows, size), BF16) for *_, size in ways for _ in range(2)
        ],
        in_specs=[pl.BlockSpec(memory_space=pltpu.SMEM)]
        + [vmem] * len(pieces)
        + [pl.BlockSpec(memory_space=pltpu.HBM)] * 4,
        out_specs=[vmem] * (2 * len(ways)),
        scratch_shapes=[
            pltpu.VMEM((n, width), BF16),
            pltpu.VMEM((n, width), F32),
            pltpu.VMEM((2, 2, width, inner), BF16),
            pltpu.VMEM((2, inner, width), BF16),
            pltpu.SemaphoreType.DMA((2, 2 * owned)),
        ],
        compiler_params=pltpu.CompilerParams(vmem_limit_bytes=VMEM_LIMIT),
        cost_estimate=pl.CostEstimate(
            flops=12 * n * owned * width * inner,
            bytes_accessed=12 * owned * width * inner + 4 * n * width,
            transcendentals=2 * n * owned * inner,
        ),
    )(first, *pieces, in_own, in_other, down_own, down_other)


HALVES = (
    ((0, ()), (1, ())),
    ((4, (0,)), (3, ())),
    ((2, ()), (5, (0,))),
    ((4, (1,)), (5, (1,))),
)
GROUPS = (
    ((0, ()),),
    ((4, (0,)),),
    ((2, ()),),
    ((4, (1,)),),
    ((1, ()),),
    ((3, ()),),
    ((5, (0,)),),
    ((5, (1,)),),
)


def plane_first(a, b):
    return a, b, over_y(a), over_x(b)


def plane_second(a, b, y_a, x_b):
    return a, b, y_a, x_b, over_x(jnp.stack([a, y_a])), over_y(jnp.stack([b, x_b]))


def partners():
    return [(3, 1)] + [(k, k + 1) for k in range(4, lax.axis_size("seq") // 2, 2)]


def gather_tokens(unit, use_halves, use_groups):
    middle = (unit.shape[1] - 128) // 2
    own = plane_first(unit[:, :middle], unit[:, middle:])
    pairs = [[across_z(unit, k) for k in pair] for pair in partners()]
    relayed = pairs[0][0]
    far_a, far_b = across_z(relayed[:, :middle], 1), across_z(relayed[:, middle:], 1)
    own = plane_second(*own)
    pairs = [plane_first(*pair) for pair in pairs]
    far_a, far_b, pairs = lax.optimization_barrier((far_a, far_b, pairs))
    far = plane_first(far_a, far_b)
    pairs = [plane_second(*pair) for pair in pairs]
    far, own = lax.optimization_barrier((far, own))
    far = plane_second(*far)
    own = use_halves(own)
    pairs, own = lax.optimization_barrier((pairs, own))
    pairs = [use_groups(pair) for pair in pairs]
    far, pairs = lax.optimization_barrier((far, pairs))
    pairs = [scatter_first(*pair) for pair in pairs]
    far = use_halves(far)
    far, pairs = lax.optimization_barrier((far, pairs))
    pairs = [scatter_second(*pair) for pair in pairs]
    far = scatter_first(*far)
    far, pairs = lax.optimization_barrier((far, pairs))
    far = scatter_second(*far)
    far, own = lax.optimization_barrier((far, own))
    return scatter_second(*scatter_first(*own)), far, pairs


def scatter_first(a_keep, a_send, b_keep, b_send):
    return add(a_keep, over_x(a_send)), add(b_keep, over_y(b_send))


def scatter_second(a, b):
    return add(a[0], over_y(a[1])), add(b[0], over_x(b[1]))


def mix(own, far, pairs):
    total = jnp.concatenate(own, 1).astype(F32)
    for pair, ways in zip(pairs, partners()):
        for part, k in zip(pair, ways):
            total = total + across_z(part, k).astype(F32)
    return (total + across_z(jnp.concatenate(far, 1), 2).astype(F32)).astype(BF16)


def shards(
    queries, keys, values, lengths, resid, w_out, moe_gain, routes, gates, w_gate_up, w_down
):
    seq, tp = lax.axis_index("seq"), lax.axis_index("tp")
    x, core, y = tp // 2, tp % 2, seq % 2
    rows = resid.shape[0]
    owned = w_gate_up.shape[0]
    count = owned * lax.axis_size("seq")

    own, other, down_other = attention(
        queries, keys, values, lengths, seq, x, core, w_down
    )
    heads = jnp.where(
        y == 0, jnp.concatenate([own, other], 1), jnp.concatenate([other, own], 1)
    )
    received = over_core(
        jnp.dot(heads[2 * rows :], w_out, preferred_element_type=F32).astype(BF16)
    )
    partial = jnp.dot(heads[: 2 * rows], w_out, preferred_element_type=F32)
    received, w_in = lax.optimization_barrier((received, w_gate_up))
    w_in = lax.optimization_barrier(w_in.transpose(0, 2, 1, 3))
    partial = partial + received.astype(F32)

    matches = routes[:, :, None] == jnp.arange(count, dtype=jnp.int32)[None, None, :]
    weight = jnp.sum(jnp.where(matches, gates[:, :, None], 0.0), axis=1)
    high = weight.astype(BF16)
    low = (weight - high.astype(F32)).astype(BF16)
    pad = -(-2 * count // 128) * 128 - 2 * count
    packed = jnp.concatenate([high, low, jnp.zeros((rows, pad), BF16)], 1)

    arrived = over_x(partial[rows:].astype(BF16))
    arrived, w_in = lax.optimization_barrier((arrived, w_in))
    weights = (w_in, over_core(w_in)), (w_down, down_other)
    attended = (resid.astype(F32) + partial[:rows] + arrived.astype(F32)).astype(BF16)
    widened = attended.astype(F32)
    meansq = jnp.mean(widened * widened, axis=1, keepdims=True)
    normed = (widened * lax.rsqrt(meansq + 1e-05) * moe_gain[None, :]).astype(BF16)

    first = (owned * seq).astype(jnp.int32).reshape(1)
    half = resid.shape[1] // 2
    halves = ((0, "x", 0, half), (0, "y", half, half))
    groups = ((0, "x", 0, 2 * half), (1, "y", 0, 2 * half))
    return attended, mix(
        *gather_tokens(
            jnp.concatenate([normed, packed], 1),
            lambda pieces: experts(first, count, pieces, HALVES, halves, weights),
            lambda pieces: experts(first, count, pieces, GROUPS, groups, weights),
        )
    )


def solution(mesh):
    return jax.shard_map(
        shards,
        mesh=mesh,
        in_specs=(
            P("seq", "tp"),
            P("seq", "tp"),
            P("seq", "tp"),
            P(),
            P(("seq", "tp"), None),
            P("tp", None),
            P(),
            P(("seq", "tp"), None),
            P(("seq", "tp"), None),
            P("seq", None, None, "tp"),
            P("seq", "tp", None),
        ),
        out_specs=(P(("seq", "tp"), None), P(("seq", "tp"), None)),
        check_vma=False,
    )
```

```python
import functools
import math

import jax
import jax.numpy as jnp
from jax import lax
from jax.experimental import pallas as pl
from jax.experimental.pallas import tpu as pltpu
from jax.sharding import PartitionSpec as P

HEAD_DIM = 128
F32 = jnp.float32
BF16 = jnp.bfloat16
VMEM_LIMIT = 20 * 1024 * 1024


def over_y(a):
    count = lax.axis_size("seq")
    return lax.ppermute(a, "seq", [(i, i ^ 1) for i in range(count)])


def over_z(a, step):
    count = lax.axis_size("seq")
    return lax.ppermute(a, "seq", [(i, (i + 2 * step) % count) for i in range(count)])


def across_z(a, k):
    count = lax.axis_size("seq")
    return lax.ppermute(a, "seq", [(i, i ^ (2 * k)) for i in range(count)])


def over_x(a):
    return lax.ppermute(a, "tp", [(i, i ^ 2) for i in range(4)])


def over_core(a):
    return lax.ppermute(a, "tp", [(i, i ^ 1) for i in range(4)])


def add(a, b):
    return (a.astype(F32) + b.astype(F32)).astype(BF16)


def relative_rows(a, x, core):
    blocks = a.reshape((2, 2, a.shape[0] // 4) + a.shape[1:])
    blocks = jnp.where(x == 0, blocks, blocks[::-1])
    blocks = jnp.where(core == 0, blocks, blocks[:, ::-1])
    return jnp.swapaxes(blocks, 0, 1).reshape(a.shape)


def attention_kernel(scale, bases, q_own, q_beside, pos_ref, start_ref, *refs):
    kv_refs, out_ref = refs[:-1], refs[-1]
    piece, width = q_own.shape
    key_pos, n = [], 0
    for kv in kv_refs:
        rows = kv.shape[0]
        column = lax.broadcasted_iota(jnp.int32, (1, rows), 1)
        if rows == piece:
            key_pos.append(column + bases[n])
            n += 1
        else:
            key_pos.append(
                jnp.where(column < piece, column + bases[n], column + (bases[n + 1] - piece))
            )
            n += 2
    for part, q_ref in enumerate((q_own, q_beside)):
        rows = pl.ds(part * piece, piece)
        pos, start = pos_ref[rows, :], start_ref[rows, :]
        masks = [(k >= start) & (k <= pos) for k in key_pos]
        for head in range(width // HEAD_DIM):
            lanes = pl.ds(head * HEAD_DIM, HEAD_DIM)
            value_lanes = pl.ds(width + head * HEAD_DIM, HEAD_DIM)
            q = q_ref[:, lanes]
            scores = [
                jnp.where(
                    mask,
                    lax.dot_general(
                        q, kv[:, lanes], (((1,), (1,)), ((), ())), preferred_element_type=F32
                    )
                    * scale,
                    -1e30,
                )
                for kv, mask in zip(kv_refs, masks)
            ]
            top = functools.reduce(jnp.maximum, [jnp.max(v, axis=1, keepdims=True) for v in scores])
            total, mixed = 0.0, 0.0
            for kv, mask, score in zip(kv_refs, masks, scores):
                weight = jnp.where(mask, jnp.exp(score - top), 0.0)
                total = total + jnp.sum(weight, axis=1, keepdims=True)
                mixed = mixed + jnp.dot(
                    weight.astype(BF16), kv[:, value_lanes], preferred_element_type=F32
                )
            out_ref[rows, lanes] = (mixed / total).astype(BF16)


def attend(q, beside, pos, start, bases, blocks):
    vmem = pl.BlockSpec(memory_space=pltpu.VMEM)
    keys = sum(b.shape[0] for b in blocks)
    return pl.pallas_call(
        functools.partial(attention_kernel, 1.0 / math.sqrt(HEAD_DIM)),
        out_shape=jax.ShapeDtypeStruct((2 * q.shape[0], q.shape[1]), BF16),
        in_specs=[pl.BlockSpec(memory_space=pltpu.SMEM)] + [vmem] * (4 + len(blocks)),
        out_specs=vmem,
        compiler_params=pltpu.CompilerParams(vmem_limit_bytes=VMEM_LIMIT),
        cost_estimate=pl.CostEstimate(
            flops=8 * q.size * keys,
            bytes_accessed=8 * q.size + 4 * keys * q.shape[1],
            transcendentals=2 * q.size // HEAD_DIM * keys,
        ),
    )(bases, q, beside, pos, start, *blocks)


def attention(queries, keys, values, lengths, seq, x, core, held):
    ring = lax.axis_size("seq") // 2
    y, z = seq % 2, seq // 2
    rows, width = queries.shape
    half = width // 2

    def split(a):
        left, right = a[:, :half], a[:, half:]
        return jnp.where(y == 0, left, right), jnp.where(y == 0, right, left)

    (k_own, k_other), (v_own, v_other) = split(keys), split(values)
    own, beside = jnp.concatenate([k_own, v_own], 1), jnp.concatenate([k_other, v_other], 1)
    own, beside, queries = lax.optimization_barrier((own, beside, queries))
    q_own, q_other = split(relative_rows(queries, x, core))
    beside = over_y(beside)
    blocks, shard = [own, beside], [2 * z + y, 2 * z + 1 - y]
    q_beside = over_y(q_other)
    for k in range(1, ring // 2 + 1):
        own = over_z(own, 1)
        if k == 1:
            own, beside = lax.optimization_barrier((own, beside))
        if k == 2:
            beside, q_beside, held = lax.optimization_barrier((beside, q_beside, held))
        beside = over_z(beside, 1)
        blocks += [own, beside]
        shard += [2 * (z - k) + y, 2 * (z - k) + 1 - y]
    bases = jnp.stack(shard).astype(jnp.int32) * rows

    local = relative_rows(jnp.arange(rows, dtype=jnp.int32), x, core)
    pos = jnp.concatenate([seq * rows + local, (seq ^ 1) * rows + local])
    bounds = jnp.cumsum(lengths)
    start = jnp.max(jnp.where(bounds[None, :] <= pos[:, None], bounds[None, :], 0), axis=1)
    blocks, held = lax.optimization_barrier((blocks, over_core(held)))
    out = attend(q_own, q_beside, pos[:, None], start[:, None], bases, blocks)
    return out[:rows], over_y(out[rows:]), held


def expert_kernel(layout, ways, count, first, *refs):
    pieces, refs = refs[: -(len(ways) * 2 + 9)], refs[-(len(ways) * 2 + 9) :]
    ins, downs = refs[:2], refs[2:4]
    outs, (tokens, total, w_in, w_down, sems) = refs[4:-5], refs[-5:]
    owned, width = ins[0].shape[0], ins[0].shape[2]
    copies = []
    for k in range(2 * owned):
        core, e = divmod(k, owned)
        copies.append(
            [
                pltpu.make_async_copy(ins[core].at[e], w_in.at[k % 2], sems.at[0, k]),
                pltpu.make_async_copy(downs[core].at[e], w_down.at[k % 2], sems.at[1, k]),
            ]
        )
        if k < 2:
            for copy in copies[-1]:
                copy.start()
    rows = pieces[0].shape[-2]
    column = lax.broadcasted_iota(jnp.int32, (1, count), 1)
    factors = [[] for _ in range(owned)]
    for i, quarter in enumerate(layout):
        at, start = pl.ds(i * rows, rows), 0
        for index, place in quarter:
            part = pieces[index].at[place] if place else pieces[index]
            size = min(part.shape[1], width - start)
            tokens[at, start : start + size] = part[:, :size]
            start += size
        packed = part[:, size:].astype(F32)
        weight = packed[:, :count] + packed[:, count : 2 * count]
        for e in range(owned):
            chosen = jnp.where(column == first[0] + e, weight, 0.0)
            factors[e].append(jnp.sum(chosen, axis=1, keepdims=True))
    factors = [jnp.concatenate(f, 0) for f in factors]
    for k in range(2 * owned):
        factor = factors[k % owned]
        copies[k][0].wait()
        gate = jnp.dot(tokens[...], w_in[k % 2, 0], preferred_element_type=F32)
        up = jnp.dot(tokens[...], w_in[k % 2, 1], preferred_element_type=F32)
        hidden = gate / (1.0 + jnp.exp(-gate)) * up * factor
        hidden = jnp.where(factor > 0, hidden, 0.0).astype(BF16)
        copies[k][1].wait()
        if k + 2 < 2 * owned:
            copies[k + 2][0].start()
        out = jnp.dot(hidden, w_down[k % 2], preferred_element_type=F32)
        if k == 0:
            total[...] = out
        else:
            total[...] += out
        if k + 2 < 2 * owned:
            copies[k + 2][1].start()
    for k, (group, by, start, size) in enumerate(ways):
        keep, send = outs[2 * k], outs[2 * k + 1]
        for i in range(4):
            at = pl.ds((4 * group + i) * rows, rows)
            y, x = divmod(i, 2)
            part = total[at, start : start + size].astype(BF16)
            if by == "x":
                (send if x else keep)[y] = part
            else:
                (send if y else keep)[x] = part


def experts(first, count, pieces, layout, ways, weights):
    (in_own, in_other), (down_own, down_other) = weights
    owned, _, width, inner = in_own.shape
    rows = pieces[0].shape[-2]
    n = len(layout) * rows
    vmem = pl.BlockSpec(memory_space=pltpu.VMEM)
    return pl.pallas_call(
        functools.partial(expert_kernel, layout, ways, count),
        out_shape=[
            jax.ShapeDtypeStruct((2, rows, size), BF16) for *_, size in ways for _ in range(2)
        ],
        in_specs=[pl.BlockSpec(memory_space=pltpu.SMEM)]
        + [vmem] * len(pieces)
        + [pl.BlockSpec(memory_space=pltpu.HBM)] * 4,
        out_specs=[vmem] * (2 * len(ways)),
        scratch_shapes=[
            pltpu.VMEM((n, width), BF16),
            pltpu.VMEM((n, width), F32),
            pltpu.VMEM((2, 2, width, inner), BF16),
            pltpu.VMEM((2, inner, width), BF16),
            pltpu.SemaphoreType.DMA((2, 2 * owned)),
        ],
        compiler_params=pltpu.CompilerParams(vmem_limit_bytes=VMEM_LIMIT),
        cost_estimate=pl.CostEstimate(
            flops=12 * n * owned * width * inner,
            bytes_accessed=12 * owned * width * inner + 4 * n * width,
            transcendentals=2 * n * owned * inner,
        ),
    )(first, *pieces, in_own, in_other, down_own, down_other)


HALVES = (
    ((0, ()), (1, ())),
    ((4, (0,)), (3, ())),
    ((2, ()), (5, (0,))),
    ((4, (1,)), (5, (1,))),
)
GROUPS = (
    ((0, ()),),
    ((4, (0,)),),
    ((2, ()),),
    ((4, (1,)),),
    ((1, ()),),
    ((3, ()),),
    ((5, (0,)),),
    ((5, (1,)),),
)


def plane_first(a, b):
    return a, b, over_y(a), over_x(b)


def plane_second(a, b, y_a, x_b):
    return a, b, y_a, x_b, over_x(jnp.stack([a, y_a])), over_y(jnp.stack([b, x_b]))


def partners():
    return [(3, 1)] + [(k, k + 1) for k in range(4, lax.axis_size("seq") // 2, 2)]


def gather_tokens(unit, use_halves, use_groups):
    middle = (unit.shape[1] - 128) // 2
    own = plane_first(unit[:, :middle], unit[:, middle:])
    pairs = [[across_z(unit, k) for k in pair] for pair in partners()]
    relayed = pairs[0][0]
    far_a, far_b = across_z(relayed[:, :middle], 1), across_z(relayed[:, middle:], 1)
    own = plane_second(*own)
    pairs = [plane_first(*pair) for pair in pairs]
    far_a, far_b, pairs = lax.optimization_barrier((far_a, far_b, pairs))
    far = plane_first(far_a, far_b)
    pairs = [plane_second(*pair) for pair in pairs]
    far, own = lax.optimization_barrier((far, own))
    far = plane_second(*far)
    own = use_halves(own)
    pairs, own = lax.optimization_barrier((pairs, own))
    pairs = [use_groups(pair) for pair in pairs]
    far, pairs = lax.optimization_barrier((far, pairs))
    pairs = [scatter_first(*pair) for pair in pairs]
    far = use_halves(far)
    far, pairs = lax.optimization_barrier((far, pairs))
    pairs = [scatter_second(*pair) for pair in pairs]
    far = scatter_first(*far)
    far, pairs = lax.optimization_barrier((far, pairs))
    far = scatter_second(*far)
    far, own = lax.optimization_barrier((far, own))
    return scatter_second(*scatter_first(*own)), far, pairs


def scatter_first(a_keep, a_send, b_keep, b_send):
    return add(a_keep, over_x(a_send)), add(b_keep, over_y(b_send))


def scatter_second(a, b):
    return add(a[0], over_y(a[1])), add(b[0], over_x(b[1]))


def mix(own, far, pairs):
    total = jnp.concatenate(own, 1).astype(F32)
    for pair, ways in zip(pairs, partners()):
        for part, k in zip(pair, ways):
            total = total + across_z(part, k).astype(F32)
    return (total + across_z(jnp.concatenate(far, 1), 2).astype(F32)).astype(BF16)


def shards(
    queries, keys, values, lengths, resid, w_out, moe_gain, routes, gates, w_gate_up, w_down
):
    seq, tp = lax.axis_index("seq"), lax.axis_index("tp")
    x, core, y = tp // 2, tp % 2, seq % 2
    rows = resid.shape[0]
    owned = w_gate_up.shape[0]
    count = owned * lax.axis_size("seq")

    own, other, down_other = attention(
        queries, keys, values, lengths, seq, x, core, w_down
    )
    heads = jnp.where(
        y == 0, jnp.concatenate([own, other], 1), jnp.concatenate([other, own], 1)
    )
    received = over_core(
        jnp.dot(heads[2 * rows :], w_out, preferred_element_type=F32).astype(BF16)
    )
    partial = jnp.dot(heads[: 2 * rows], w_out, preferred_element_type=F32)
    received, w_in = lax.optimization_barrier((received, w_gate_up))
    w_in = lax.optimization_barrier(w_in.transpose(0, 2, 1, 3))
    partial = partial + received.astype(F32)

    matches = routes[:, :, None] == jnp.arange(count, dtype=jnp.int32)[None, None, :]
    weight = jnp.sum(jnp.where(matches, gates[:, :, None], 0.0), axis=1)
    high = weight.astype(BF16)
    low = (weight - high.astype(F32)).astype(BF16)
    pad = -(-2 * count // 128) * 128 - 2 * count
    packed = jnp.concatenate([high, low, jnp.zeros((rows, pad), BF16)], 1)

    arrived = over_x(partial[rows:].astype(BF16))
    arrived, w_in = lax.optimization_barrier((arrived, w_in))
    weights = (w_in, over_core(w_in)), (w_down, down_other)
    attended = (resid.astype(F32) + partial[:rows] + arrived.astype(F32)).astype(BF16)
    widened = attended.astype(F32)
    meansq = jnp.mean(widened * widened, axis=1, keepdims=True)
    normed = (widened * lax.rsqrt(meansq + 1e-05) * moe_gain[None, :]).astype(BF16)

    first = (owned * seq).astype(jnp.int32).reshape(1)
    half = resid.shape[1] // 2
    halves = ((0, "x", 0, half), (0, "y", half, half))
    groups = ((0, "x", 0, 2 * half), (1, "y", 0, 2 * half))
    return attended, mix(
        *gather_tokens(
            jnp.concatenate([normed, packed], 1),
            lambda pieces: experts(first, count, pieces, HALVES, halves, weights),
            lambda pieces: experts(first, count, pieces, GROUPS, groups, weights),
        )
    )


def solution(mesh):
    return jax.shard_map(
        shards,
        mesh=mesh,
        in_specs=(
            P("seq", "tp"),
            P("seq", "tp"),
            P("seq", "tp"),
            P(),
            P(("seq", "tp"), None),
            P("tp", None),
            P(),
            P(("seq", "tp"), None),
            P(("seq", "tp"), None),
            P("seq", None, None, "tp"),
            P("seq", "tp", None),
        ),
        out_specs=(P(("seq", "tp"), None), P(("seq", "tp"), None)),
        check_vma=False,
    )
```
